512 devices in a mesh: rep: 8 (over z_hi, core), ep: 64 (over x, y, z_lo).
Axes of the slice: x: 4, y: 4, z: 16 (z_hi: 4, z_lo: 4; z = z_hi * 4 + z_lo), core: 2. Of those that a mesh axis runs over, the one named last changes fastest.
Arguments:
- rows_old: bfloat16 [2048, 3584], P('ep'), may hold values from -6 to 6
- rows_new: bfloat16 [2048, 3584], P('ep'), may hold values from -6 to 6
- routes_old: int32 [2048, 8], P('ep'), may hold values from 0 to 63, all different within a row; in each aligned block of 32 rows (0 to 31, 32 to 63, ...) at most 6 rows name the same one
- routes_new: int32 [2048, 8], P('ep'), may hold values from 0 to 63, all different within a row; in each aligned block of 32 rows (0 to 31, 32 to 63, ...) at most 6 rows name the same one
- gates_old: float32 [2048, 8], P('ep'), may hold values from 0.05 to 0.5
- gates_new: float32 [2048, 8], P('ep'), may hold values from 0.05 to 0.5
- w_in_old: bfloat16 [64, 3584, 2, 1024], P('ep', None, None, 'rep'), may hold values from -0.09375 to 0.09375
- w_in_new: bfloat16 [64, 3584, 2, 1024], P('ep', 'rep'), may hold values from -0.09375 to 0.09375
- w_out: bfloat16 [64, 1024, 3584], P('ep', 'rep'), may hold values from -0.1875 to 0.1875
Outputs:
- out_old: bfloat16 [2048, 3584], P('ep', 'rep')
- out_new: bfloat16 [2048, 3584], P('ep', 'rep')
The draws below stay inside these ranges and needn't reach their ends.
Inputs may be any that keep to these rules, and one draw needn't show every extreme that they name: `routes_old`: each row names 8 different experts; within the 32 rows of one device no expert is named more than 6 times. `routes_new`: each row names 8 different experts; within the 32 rows of one device no expert is named more than 6 times.
All inputs are finite; a program needn't handle non-finite values.
Results may differ from the reference program's by a relative error of at most 0.02.
Values may be sent and summed in bfloat16 or wider, within the bound.
A program may use at most 64 MiB of HBM per device.

```python
import math
import jax
import jax.numpy as jnp
import numpy as np
from jax import lax

D = 3584
H = 1024
TOPK = 8
ROW_DEV = 32
EXPERTS = 64
CAP = 6
ROWS = 2048
N_REP = 8
N_EP = 64


def block_levels(key, shape, shards, smallest, largest):
    level, own = 1.0, jax.random.fold_in(key, 6)
    for dim, shards_of in shards:
        heights = jnp.exp(jax.random.uniform(jax.random.fold_in(own, dim), (shards_of,), jnp.float32, smallest / len(shards), largest / len(shards)))
        level = level * jnp.repeat(heights, shape[dim] // shards_of).reshape([-1 if axis == dim else 1 for axis in range(len(shape))])
    return level


def assign_block(key, own, number, rows, number_of, top, reach, lean):
    ranking = jax.random.permutation(key, number_of)
    crowded, usual = shares(number_of, rows * top, reach, lean, True), shares(number_of, rows * top, reach, lean, False)
    places = jnp.arange(number_of)

    def named(sizes, turn):
        used = int((sizes > 0).sum())
        fixed = max(1, used // 4)
        moved = fixed + (places - fixed + turn * (used - fixed)) % max(1, number_of - fixed)
        return jnp.zeros((number_of,), jnp.int32).at[ranking[jnp.where(places < fixed, places, moved)]].set(jnp.asarray(sizes, jnp.int32))

    sizes = jnp.where(number % 4 == 0, named(crowded, number // 4), named(usual, number - number // 4 - 1))
    mixed = jax.random.permutation(jax.random.fold_in(own, 3), number_of)
    source_of, receiver = mixed[0:number_of // 2 * 2:2], mixed[1:number_of // 2 * 2:2]
    slack = jnp.minimum(sizes[source_of] - 1, reach - sizes[receiver]) // 2
    slack = jnp.where((source_of == ranking[0]) | (receiver == ranking[0]) | (sizes[receiver] == 0), 0, jnp.maximum(slack, 0))
    moved = jax.random.randint(jax.random.fold_in(own, 4), (number_of // 2,), 0, 1 << 20) % (slack + 1)
    sizes = sizes.at[source_of].add(-moved).at[receiver].add(moved)
    members = jnp.searchsorted(jnp.cumsum(sizes), jnp.arange(rows * top), side="right").astype(jnp.int32)
    table = members.reshape(top, rows).T
    table = table[jax.random.permutation(jax.random.fold_in(own, 1), rows)]
    turn = jax.random.randint(jax.random.fold_in(own, 2), (rows, 1), 0, top)
    return jnp.take_along_axis(table, (jnp.arange(top)[None, :] + turn) % top, axis=1)


def shares(number_of, total, limit, lean, full):
    loads = [(1 << 20) // math.isqrt(standing ** lean) + 1 for standing in range(1, number_of + 1)]
    largest = limit if full else min(limit, max(-(-total // number_of), total * loads[0] // sum(loads)))
    least = 1 if total - largest >= number_of - 1 else 0
    holding, rest = [largest] + [least] * (number_of - 1), total - largest - least * (number_of - 1)
    while rest > 0:
        candidates = [i for i in range(1, number_of) if holding[i] < largest] or [i for i in range(1, number_of) if holding[i] < limit]
        pool, left = sum([loads[i] for i in candidates]), rest
        for i in candidates:
            more = min(limit - holding[i], max(1, left * loads[i] // pool), rest)
            holding[i] = holding[i] + more
            rest = rest - more
    return np.array(holding)


def gaussian(stream_key, dims, width, most, pieces=(), kind=jnp.bfloat16):
    entries = width * jax.random.normal(stream_key, dims, jnp.float32)
    if pieces:
        entries = entries * block_levels(stream_key, dims, pieces, -0.22, 0.18)
    return jnp.clip(entries, -most, most).astype(kind)


def setup_inputs(seed: int = 0) -> dict:
    arg_keys = jax.random.split(jax.random.key(seed), 10)
    rows_old = gaussian(arg_keys[0], (ROWS, D), 1.0, 6.0, ((0, 64),))
    rows_new = gaussian(arg_keys[1], (ROWS, D), 1.0, 6.0, ((0, 64),))
    routes_old_keys = jax.random.split(jax.random.fold_in(arg_keys[2], 1), ROWS // ROW_DEV)
    routes_old_turns = jax.random.permutation(jax.random.fold_in(arg_keys[2], 3), ROWS // ROW_DEV)
    routes_old = jax.vmap(lambda own, number: assign_block(jax.random.fold_in(arg_keys[2], 2), own, number, ROW_DEV, EXPERTS, TOPK, CAP, 2))(routes_old_keys, routes_old_turns).reshape((ROWS, TOPK))
    routes_new_keys = jax.random.split(jax.random.fold_in(arg_keys[3], 1), ROWS // ROW_DEV)
    routes_new_turns = jax.random.permutation(jax.random.fold_in(arg_keys[3], 3), ROWS // ROW_DEV)
    routes_new = jax.vmap(lambda own, number: assign_block(jax.random.fold_in(arg_keys[3], 2), own, number, ROW_DEV, EXPERTS, TOPK, CAP, 2))(routes_new_keys, routes_new_turns).reshape((ROWS, TOPK))
    gates_old = jnp.clip(jnp.exp(math.log(0.5) - 2.3025851 * jax.random.uniform(arg_keys[4], (ROWS, TOPK), jnp.float32) ** block_levels(arg_keys[4], (ROWS, TOPK), ((0, 64),), -0.2, 0.2)), 0.05, 0.5)
    gates_new = jnp.clip(jnp.exp(math.log(0.5) - 2.3025851 * jax.random.uniform(arg_keys[5], (ROWS, TOPK), jnp.float32) ** block_levels(arg_keys[5], (ROWS, TOPK), ((0, 64),), -0.2, 0.2)), 0.05, 0.5)
    w_in_old = gaussian(arg_keys[6], (EXPERTS, D, 2, H), D ** -0.5, 0.09375, ((0, 64), (3, 8)))
    w_in_new = gaussian(arg_keys[7], (EXPERTS, D, 2, H), D ** -0.5, 0.09375, ((0, 64), (1, 8)))
    w_out = gaussian(arg_keys[8], (EXPERTS, H, D), H ** -0.5, 0.1875, ((0, 64), (1, 8)))
    return {"rows_old": rows_old, "rows_new": rows_new, "routes_old": routes_old, "routes_new": routes_new, "gates_old": gates_old, "gates_new": gates_new, "w_in_old": w_in_old, "w_in_new": w_in_new, "w_out": w_out}


def slot_table(routing, capacity, count):
    flattened = routing.reshape(-1)
    onehot = (flattened[:, None] == jnp.arange(count, dtype=jnp.int32)[None, :]).astype(jnp.int32)
    before = jnp.cumsum(onehot, axis=0) - onehot
    slot_rank = jnp.sum(before * onehot, axis=1)
    return (flattened * capacity + slot_rank).astype(jnp.int32)


def source_rows(positions, topk, capacity, count):
    pair_index = jnp.arange(positions.shape[0], dtype=jnp.int32)
    sources = jnp.zeros((count * capacity,), jnp.int32).at[positions].set(pair_index // topk)
    filled = jnp.zeros((count * capacity,), jnp.int32).at[positions].set(1)
    return sources, filled


def moe_layer(tokens, routing, gates, w_in, w_out):
    blocks = tokens.reshape(N_EP, ROW_DEV, D)
    routed = routing.reshape(N_EP, ROW_DEV, TOPK)
    positions = jax.vmap(lambda r: slot_table(r, CAP, EXPERTS))(routed)
    sources, filled = jax.vmap(lambda p: source_rows(p, TOPK, CAP, EXPERTS))(positions)
    buffers = jnp.take_along_axis(blocks, sources[:, :, None], axis=1)
    buffers = buffers * filled[:, :, None].astype(tokens.dtype)
    buffers = jnp.transpose(buffers.reshape(N_EP, EXPERTS, CAP, D), (1, 0, 2, 3))
    slab = H // N_REP

    def expert_work(operands):
        buffer, weights_in, weights_out = operands
        act = jnp.einsum("bcd,dgh->bcgh", buffer.astype(jnp.float32), weights_in.astype(jnp.float32))
        hidden = (jax.nn.silu(act[:, :, 0]) * act[:, :, 1]).astype(jnp.bfloat16)
        split = hidden.reshape(N_EP, CAP, N_REP, slab).astype(jnp.float32)
        down = weights_out.reshape(N_REP, slab, D).astype(jnp.float32)
        partial_value = jnp.einsum("bcrh,rhd->bcrd", split, down).astype(jnp.bfloat16)
        return jnp.sum(partial_value.astype(jnp.float32), axis=2)

    results = lax.map(expert_work, (buffers, w_in, w_out))
    results = jnp.transpose(results, (1, 0, 2, 3)).reshape(N_EP, EXPERTS * CAP, D)
    gathered = jnp.take_along_axis(results, positions[:, :, None], axis=1)
    gathered = gathered.reshape(N_EP, ROW_DEV, TOPK, D)
    weights = gates.reshape(N_EP, ROW_DEV, TOPK).astype(jnp.float32)
    combined = jnp.einsum("brk,brkd->brd", weights, gathered)
    return combined.reshape(ROWS, D).astype(jnp.bfloat16)


def reference(rows_old, rows_new, routes_old, routes_new, gates_old, gates_new, w_in_old, w_in_new, w_out):
    out_old = moe_layer(rows_old, routes_old, gates_old, w_in_old, w_out)
    out_new = moe_layer(rows_new, routes_new, gates_new, w_in_new, w_out)
    return out_old, out_new
```

```python
import functools

import jax
import jax.numpy as jnp
from jax import lax
from jax.experimental import pallas as pl
from jax.experimental.pallas import tpu as pltpu
from jax.sharding import PartitionSpec as P

BF = jnp.bfloat16
F32 = jnp.float32
MESH = pl.DeviceIdType.MESH

D = 3584
HALF = D // 2
BLK = HALF // 2
WIN = 512
SLICE = 448
SLAB = 128
TOPK = 8
ROWS = 32
CAP = 6
SLOTS = 4 * CAP
CH = 4 * SLOTS
ORDER = (2, 1, 3, 0)
ZOFF = (1, 15, 2)


def dot(a, b):
    return lax.dot_general(a, b, (((1,), (0,)), ((), ())), preferred_element_type=F32)


def dot_nt(a, b):
    return lax.dot_general(a, b, (((1,), (1,)), ((), ())), preferred_element_type=F32)


def iota(shape, dim):
    return lax.broadcasted_iota(jnp.int32, shape, dim)


def by24(q):
    return (q * 2731) >> 16


def by6(q):
    return (q * 10923) >> 16


def kernel(
    meta, rows_old, rows_new, w_old, w_new, w_out,
    out_old, out_new,
    meta_z, rz_old, rz_new, disp, comb,
    send_new, recv_new, send_old, recv_old, sib_old,
    pn_own, sx_send, sx_recv, rs_send, rs_recv,
    po, so_send, so_recv, ret_send, ret_recv,
    z1_own, z1_send, z1_recv, z2_send, z2_recv,
    zs, zr, xs, xr, fs, fr, sxs, sxr, rss, rsr, sos, sor, rts, rtr, z1s, z1r, z2s, z2r,
):
    ep = lax.axis_index("ep")
    rep = lax.axis_index("rep")
    core, zh = lax.rem(rep, 2), rep // 2
    zl, me = lax.rem(ep, 4), ep // 4
    x, y = me // 4, lax.rem(me, 4)
    z = zh * 4 + zl

    def z_dev(offset):
        t = lax.rem(z + offset, 16)
        return {"rep": (t // 4) * 2 + core, "ep": me * 4 + lax.rem(t, 4)}

    def peer(dx, dy):
        return lax.rem(x + dx, 4) * 4 + lax.rem(y + dy, 4)

    def xy_dev(d):
        return {"rep": rep, "ep": d * 4 + zl}

    def zh_dev(k):
        return {"rep": lax.rem(zh + k, 4) * 2 + core, "ep": ep}

    sibling = {"rep": zh * 2 + (1 - core), "ep": ep}

    def remote(src, dst, ss, rs, dev):
        return pltpu.make_async_remote_copy(
            src_ref=src, dst_ref=dst, send_sem=ss, recv_sem=rs, device_id=dev, device_id_type=MESH
        )

    barrier = pltpu.get_barrier_semaphore()
    for i in range(1, 16):
        pl.semaphore_signal(barrier, 1, device_id=xy_dev(peer(i // 4, i % 4)), device_id_type=MESH)
    for o in (1, 15, 2, 14):
        pl.semaphore_signal(barrier, 1, device_id=z_dev(o), device_id_type=MESH)
    for k in range(1, 8):
        pl.semaphore_signal(
            barrier, 1, device_id={"rep": lax.rem(rep + k, 8), "ep": ep}, device_id_type=MESH
        )
    half = pl.multiple_of(core * HALF, 128)
    other = pl.multiple_of((1 - core) * HALF, 128)
    mine = pl.ds(pl.multiple_of(zl * ROWS, ROWS), ROWS)
    meta_z[mine, :] = meta[...]
    rz_old[mine, :] = rows_old[:, pl.ds(half, HALF)]
    rz_new[mine, :] = rows_new[:, pl.ds(pl.multiple_of(zh * 896 + core * 384, 128), WIN)]
    pl.semaphore_wait(barrier, 26)

    def z_copy(o, kind):
        offset = ZOFF[o]
        there = lax.rem(z + offset, 16) // 4
        if kind == 0:
            src, land = meta, meta_z
        elif kind == 1:
            window = pl.ds(pl.multiple_of(there * 896 + core * 384, 128), WIN)
            src, land = rows_new.at[:, window], rz_new
        else:
            src, land = rows_old.at[:, pl.ds(half, HALF)], rz_old
        return remote(src, land.at[mine, :], zs.at[kind, o], zr.at[kind, o], z_dev(offset))

    def z_from(o, kind, buf):
        src = lax.rem(zl + 16 - ZOFF[o], 4)
        ref = buf.at[pl.ds(pl.multiple_of(src * ROWS, ROWS), ROWS), :]
        return remote(ref, ref, zs.at[kind, o], zr.at[kind, o], z_dev(ZOFF[o]))

    for kind in range(3):
        for o in range(3):
            z_copy(o, kind).start()
    for o in range(3):
        z_from(o, 0, meta_z).wait_recv()

    lane = iota((4 * ROWS, 128), 1)
    p_row, p_col = iota((4 * ROWS, 4 * ROWS), 0), iota((4 * ROWS, 4 * ROWS), 1)
    before = jnp.where((p_col < p_row) & (p_col >> 5 == p_row >> 5), 1.0, 0.0).astype(BF)
    qs = iota((16 * SLOTS, 128), 0)
    pick = jnp.where(by24(qs) * 4 + zl == iota((16 * SLOTS, 128), 1), 1.0, 0.0).astype(BF)
    in_q = qs - by24(qs) * 24
    slot_q = (in_q - by6(in_q) * 6).astype(F32)
    same_q = by6(in_q) == iota((16 * SLOTS, 128), 1) >> 5
    ql = iota((128, 16 * SLOTS), 1)
    in_l = ql - by24(ql) * 24
    slot_l = (in_l - by6(in_l) * 6).astype(F32)
    same_l = by6(in_l) == iota((128, 16 * SLOTS), 0) >> 5
    for b in range(2):
        named = jnp.zeros((4 * ROWS, 128), F32)
        gate = jnp.zeros((4 * ROWS, 128), F32)
        for k in range(TOPK):
            hit = meta_z[:, 8 * b + k : 8 * b + k + 1].astype(jnp.int32) == lane
            named = named + jnp.where(hit, 1.0, 0.0)
            gate = gate + jnp.where(hit, meta_z[:, 16 + 8 * b + k : 17 + 8 * b + k], 0.0)
        rank = dot(before, named.astype(BF))
        code = jnp.where(named > 0.5, rank, -1.0).astype(BF)
        disp[b] = jnp.where((dot_nt(pick, code) == slot_q) & same_q, 1.0, 0.0).astype(BF)
        chosen = (dot_nt(code, pick) == slot_l) & same_l
        high = gate.astype(BF)
        low = (gate - high.astype(F32)).astype(BF)
        comb[b, 0] = jnp.where(chosen, dot_nt(high, pick), 0.0).astype(BF)
        comb[b, 1] = jnp.where(chosen, dot_nt(low, pick), 0.0).astype(BF)

    def message_to(b, buf, land, dx, dy):
        d = peer(dx, dy)
        i = 4 * dx + dy
        return remote(buf.at[d], land.at[me], xs.at[b, i], xr.at[b, i], xy_dev(d))

    def message_from(b, land, dx, dy):
        d = peer(4 - dx, 4 - dy)
        i = 4 * dx + dy
        return d, remote(land.at[d], land.at[d], xs.at[b, i], xr.at[b, i], xy_dev(d))

    def put(buf, at, value, width):
        v = value.reshape(4, SLOTS, 2 * width)
        buf[at, 0:SLOTS, :] = v[:, :, :width].astype(BF)
        buf[at, SLOTS : 2 * SLOTS, :] = v[:, :, width:].astype(BF)

    def take(buf, g, h, width):
        v = buf[pl.ds(4 * g, 4), h * SLOTS : (h + 1) * SLOTS, :]
        return v.astype(F32).reshape(CH, width).astype(BF)

    def dispatch(b, rz, buf, land, width):
        for s in ORDER:
            g = lax.rem(x + s, 4)
            table = disp[b, pl.ds(pl.multiple_of(g * CH, 16), CH), :]
            put(buf, pl.ds(4 * g, 4), dot(table, rz[...]), width)
            for dy in (2, 1, 3, 0):
                if (s, dy) == (0, 0):
                    land[me] = buf[me]
                else:
                    message_to(b, buf, land, s, dy).start()

    for o in range(3):
        z_from(o, 1, rz_new).wait_recv()
    dispatch(1, rz_new, send_new, recv_new, WIN // 2)
    for o in range(3):
        z_from(o, 2, rz_old).wait_recv()
    dispatch(0, rz_old, send_old, recv_old, BLK)

    def sx_copy(s):
        return remote(sx_send.at[s], sx_recv.at[s], sxs.at[s], sxr.at[s], sibling)

    def rs_copy(s, k):
        return remote(
            rs_send.at[s, lax.rem(zh + k, 4)], rs_recv.at[s, k - 1],
            rss.at[s, k - 1], rsr.at[s, k - 1], zh_dev(k),
        )

    def act_part(s):
        g = lax.rem(x + 4 - s, 4)
        for dy in (2, 1, 3, 0):
            if (s, dy) != (0, 0):
                message_from(1, recv_new, s, dy)[1].wait_recv()
        rows = [take(recv_new, g, h, WIN // 2) for h in range(2)]

        def part(c):
            return sum(dot(rows[h], w_new[c, h * (WIN // 2) : (h + 1) * (WIN // 2), :]) for h in range(2))

        sx_send[s] = part(1 - core).astype(BF)
        sx_copy(s).start()
        pn_own[s] = part(core)

    def act_send(s):
        sx_copy(s).wait_recv()
        for k in range(4):
            cols = slice(256 * k, 256 * (k + 1))
            rs_send[s, k] = (pn_own[s, :, cols] + sx_recv[s, :, cols].astype(F32)).astype(BF)
        for k in (2, 1, 3):
            rs_copy(s, k).start()

    def so_copy(b, s):
        return remote(so_send.at[b, s], so_recv.at[b, s], sos.at[b, s], sor.at[b, s], sibling)

    def down(b, s, act):
        gate = act[:, :SLAB]
        hidden = (gate / (1.0 + jnp.exp(-gate)) * act[:, SLAB:]).astype(BF)
        so_send[b, s] = dot(hidden, w_out[:, pl.ds(other, HALF)]).astype(BF)
        so_copy(b, s).start()
        po[b, s] = dot(hidden, w_out[:, pl.ds(half, HALF)])

    def back_to(b, dx, dy):
        d = peer(4 - dx, 4 - dy)
        i = 4 * dx + dy
        return remote(ret_send.at[b, d], ret_recv.at[b, me], rts.at[b, i], rtr.at[b, i], xy_dev(d))

    def back_from(b, dx, dy):
        d = peer(dx, dy)
        i = 4 * dx + dy
        return remote(ret_send.at[b, d], ret_recv.at[b, d], rts.at[b, i], rtr.at[b, i], xy_dev(d))

    def back(b, s):
        g = lax.rem(x + 4 - s, 4)
        so_copy(b, s).wait_recv()
        put(ret_send.at[b], pl.ds(4 * g, 4), po[b, s] + so_recv[b, s].astype(F32), BLK)
        for dy in (2, 1, 3, 0):
            if (s, dy) == (0, 0):
                ret_recv[b, me] = ret_send[b, me]
            else:
                back_to(b, s, dy).start()

    for n in range(5):
        if n < 4:
            act_part(ORDER[n])
        if n >= 1:
            act_send(ORDER[n - 1])

    def fwd_copy(s, dy):
        d = peer(4 - s, 4 - dy)
        i = 4 * s + dy
        return remote(recv_old.at[d], sib_old.at[d], fs.at[i], fr.at[i], sibling)

    def forward(s):
        for dy in (2, 1, 3, 0):
            if (s, dy) != (0, 0):
                message_from(0, recv_old, s, dy)[1].wait_recv()
            fwd_copy(s, dy).start()

    def act_old(s):
        g = lax.rem(x + 4 - s, 4)
        act = jnp.zeros((CH, 2 * SLAB), F32)
        for h in range(2):
            at = pl.ds(pl.multiple_of(half + h * BLK, 128), BLK)
            act += dot(take(recv_old, g, h, BLK), w_old[at, :])
        for dy in range(4):
            fwd_copy(s, dy).wait_recv()
        for h in range(2):
            at = pl.ds(pl.multiple_of(other + h * BLK, 128), BLK)
            act += dot(take(sib_old, g, h, BLK), w_old[at, :])
        down(0, s, act)

    for n in range(6):
        if n < 4:
            forward(ORDER[n])
        if 1 <= n < 5:
            act_old(ORDER[n - 1])
        if n >= 2:
            back(0, ORDER[n - 2])

    def act_new(s):
        act = rs_send[s, zh].astype(F32)
        for k in range(1, 4):
            rs_copy(s, k).wait_recv()
            act += rs_recv[s, k - 1].astype(F32)
        down(1, s, act)

    for n in range(5):
        if n < 4:
            act_new(ORDER[n])
        if n >= 1:
            back(1, ORDER[n - 1])

    def z1_copy(b, o):
        at = pl.ds(pl.multiple_of(lax.rem(zl + ZOFF[o], 4) * ROWS, ROWS), ROWS)
        return remote(z1_send.at[b, at, :], z1_recv.at[b, o], z1s.at[b, o], z1r.at[b, o], z_dev(ZOFF[o]))

    def combine(b):
        for i in range(1, 16):
            back_from(b, i // 4, i % 4).wait_recv()
        for h in range(2):
            rows = ret_recv[b, :, h * SLOTS : (h + 1) * SLOTS, :]
            rows = rows.astype(F32).reshape(16 * SLOTS, BLK).astype(BF)
            total = dot(comb[b, 0], rows) + dot(comb[b, 1], rows)
            cols = slice(h * BLK, (h + 1) * BLK)
            z1_own[b, :, cols] = total
            z1_send[b, :, cols] = total.astype(BF)
        for o in range(3):
            z1_copy(b, o).start()

    def z2_copy(b, t):
        k, c = t // 2, t % 2
        return remote(
            z2_send.at[b, :, k * 896 + c * 384 : k * 896 + c * 384 + WIN], z2_recv.at[b, zh],
            z2s.at[b, t], z2r.at[b, zh], {"rep": (2 * core + k) * 2 + c, "ep": ep},
        )

    def is_self(t):
        return rep == (2 * core + t // 2) * 2 + t % 2

    def spread(b):
        total = z1_own[b, mine, :]
        for o in range(3):
            z1_copy(b, o).wait_recv()
            total += z1_recv[b, o].astype(F32)
        z2_send[b] = total.astype(BF)
        for t in range(4):
            k, c = t // 2, t % 2

            @pl.when(jnp.logical_not(is_self(t)))
            def _():
                z2_copy(b, t).start()

            @pl.when(is_self(t))
            def _():
                z2_recv[b, zh] = z2_send[b, :, k * 896 + c * 384 : k * 896 + c * 384 + WIN]

    def finish(b, out):
        for s in range(4):

            @pl.when(jnp.logical_not((zh == s) & (core == zh // 2)))
            def _():
                ref = z2_recv.at[b, s]
                remote(ref, ref, z2s.at[b, 0], z2r.at[b, s], sibling).wait_recv()

        total = sum(z2_recv[b, s].astype(F32) for s in range(4))
        out[...] = jnp.where(core == 0, total[:, :SLICE], total[:, WIN - SLICE :]).astype(BF)

    combine(0)
    spread(0)
    combine(1)
    finish(0, out_old)
    spread(1)
    finish(1, out_new)

    for o in range(3):
        for kind in range(3):
            z_copy(o, kind).wait_send()
        for b in range(2):
            z1_copy(b, o).wait_send()
    for s in range(4):
        sx_copy(s).wait_send()
        for k in range(1, 4):
            rs_copy(s, k).wait_send()
        for dy in range(4):
            fwd_copy(s, dy).wait_send()
        for b in range(2):
            so_copy(b, s).wait_send()
            for dy in range(4):
                if (s, dy) != (0, 0):
                    message_to(b, (send_old, send_new)[b], (recv_old, recv_new)[b], s, dy).wait_send()
                    back_to(b, s, dy).wait_send()
    for b in range(2):
        for t in range(4):

            @pl.when(jnp.logical_not(is_self(t)))
            def _():
                z2_copy(b, t).wait_send()


def body(rows_old, rows_new, routes_old, routes_new, gates_old, gates_new, w_in_old, w_in_new, w_out):
    core = lax.rem(lax.axis_index("rep"), 2)
    meta = jnp.concatenate(
        [routes_old.astype(F32), routes_new.astype(F32), gates_old, gates_new], axis=1
    )
    meta = jnp.pad(meta, ((0, 0), (0, 96)))
    w_old = w_in_old[0].reshape(D, 2 * SLAB)
    w_new = w_in_new[0].reshape(SLICE, 2, 4, 2, SLAB).transpose(3, 0, 2, 1, 4).reshape(2, SLICE, 1024)
    pad = WIN - SLICE
    w_new = jnp.where(
        core == 0, jnp.pad(w_new, ((0, 0), (0, pad), (0, 0))), jnp.pad(w_new, ((0, 0), (pad, 0), (0, 0)))
    )
    vmem = pl.BlockSpec(memory_space=pltpu.VMEM)
    dma = pltpu.SemaphoreType.DMA
    out = jax.ShapeDtypeStruct((ROWS, SLICE), BF)
    return pl.pallas_call(
        kernel,
        out_shape=(out, out),
        in_specs=[vmem] * 6,
        out_specs=(vmem, vmem),
        scratch_shapes=[
            pltpu.VMEM((4 * ROWS, 128), F32),
            pltpu.VMEM((4 * ROWS, HALF), BF),
            pltpu.VMEM((4 * ROWS, WIN), BF),
            pltpu.VMEM((2, 16 * SLOTS, 128), BF),
            pltpu.VMEM((2, 2, 128, 16 * SLOTS), BF),
            pltpu.VMEM((16, 2 * SLOTS, WIN // 2), BF),
            pltpu.VMEM((16, 2 * SLOTS, WIN // 2), BF),
            pltpu.VMEM((16, 2 * SLOTS, BLK), BF),
            pltpu.VMEM((16, 2 * SLOTS, BLK), BF),
            pltpu.VMEM((16, 2 * SLOTS, BLK), BF),
            pltpu.VMEM((4, CH, 1024), F32),
            pltpu.VMEM((4, CH, 1024), BF),
            pltpu.VMEM((4, CH, 1024), BF),
            pltpu.VMEM((4, 4, CH, 256), BF),
            pltpu.VMEM((4, 3, CH, 256), BF),
            pltpu.VMEM((2, 4, CH, HALF), F32),
            pltpu.VMEM((2, 4, CH, HALF), BF),
            pltpu.VMEM((2, 4, CH, HALF), BF),
            pltpu.VMEM((2, 16, 2 * SLOTS, BLK), BF),
            pltpu.VMEM((2, 16, 2 * SLOTS, BLK), BF),
            pltpu.VMEM((2, 4 * ROWS, HALF), F32),
            pltpu.VMEM((2, 4 * ROWS, HALF), BF),
            pltpu.VMEM((2, 3, ROWS, HALF), BF),
            pltpu.VMEM((2, ROWS, HALF), BF),
            pltpu.VMEM((2, 4, ROWS, WIN), BF),
            dma((3, 3)), dma((3, 3)),
            dma((2, 16)), dma((2, 16)),
            dma((16,)), dma((16,)),
            dma((4,)), dma((4,)),
            dma((4, 3)), dma((4, 3)),
            dma((2, 4)), dma((2, 4)),
            dma((2, 16)), dma((2, 16)),
            dma((2, 3)), dma((2, 3)),
            dma((2, 4)), dma((2, 4)),
        ],
        compiler_params=pltpu.CompilerParams(
            collective_id=0, has_side_effects=True, vmem_limit_bytes=60 * 1024 * 1024
        ),
    )(meta, rows_old, rows_new, w_old, w_new, w_out[0])


def solution(mesh):
    return jax.shard_map(
        body,
        mesh=mesh,
        in_specs=(
            P("ep", None),
            P("ep", None),
            P("ep", None),
            P("ep", None),
            P("ep", None),
            P("ep", None),
            P("ep", None, None, "rep"),
            P("ep", "rep", None, None),
            P("ep", "rep", None),
        ),
        out_specs=(P("ep", "rep"), P("ep", "rep")),
        check_vma=False,
    )
```

```python
import functools

import jax
import jax.numpy as jnp
from jax import lax
from jax.experimental import pallas as pl
from jax.experimental.pallas import tpu as pltpu
from jax.sharding import PartitionSpec as P

BF = jnp.bfloat16
F32 = jnp.float32
MESH = pl.DeviceIdType.MESH

D = 3584
HALF = D // 2
BLK = HALF // 2
WIN = 512
SLICE = 448
SLAB = 128
TOPK = 8
ROWS = 32
CAP = 6
SLOTS = 4 * CAP
CH = 4 * SLOTS
ORDER = (2, 1, 3, 0)
ZOFF = (1, 15, 2)


def dot(a, b):
    return lax.dot_general(a, b, (((1,), (0,)), ((), ())), preferred_element_type=F32)


def dot_nt(a, b):
    return lax.dot_general(a, b, (((1,), (1,)), ((), ())), preferred_element_type=F32)


def iota(shape, dim):
    return lax.broadcasted_iota(jnp.int32, shape, dim)


def by24(q):
    return (q * 2731) >> 16


def by6(q):
    return (q * 10923) >> 16


def kernel(
    ro_t, rn_t, go_t, gn_t, rows_old, rows_new, w_old_hbm, w_new_hbm, w_out_hbm,
    out_old, out_new,
    w_raw, w_wide, w_old, w_new, w_out, square, meta_z, rz_old, rz_new, disp, comb,
    send_new, recv_new, send_old, recv_old, sib_old,
    pn_own, sx_send, sx_recv, rs_send, rs_recv,
    po, so_send, so_recv, ret_send, ret_recv,
    z1_own, z1_send, z1_recv, z2_send, z2_recv,
    ws, zs, zr, xs, xr, fs, fr, sxs, sxr, rss, rsr, sos, sor, rts, rtr, z1s, z1r, z2s, z2r,
):
    ep = lax.axis_index("ep")
    rep = lax.axis_index("rep")
    core, zh = lax.rem(rep, 2), rep // 2
    zl, me = lax.rem(ep, 4), ep // 4
    x, y = me // 4, lax.rem(me, 4)
    z = zh * 4 + zl

    def z_dev(offset):
        t = lax.rem(z + offset, 16)
        return {"rep": (t // 4) * 2 + core, "ep": me * 4 + lax.rem(t, 4)}

    def peer(dx, dy):
        return lax.rem(x + dx, 4) * 4 + lax.rem(y + dy, 4)

    def xy_dev(d):
        return {"rep": rep, "ep": d * 4 + zl}

    def zh_dev(k):
        return {"rep": lax.rem(zh + k, 4) * 2 + core, "ep": ep}

    sibling = {"rep": zh * 2 + (1 - core), "ep": ep}

    def remote(src, dst, ss, rs, dev):
        return pltpu.make_async_remote_copy(
            src_ref=src, dst_ref=dst, send_sem=ss, recv_sem=rs, device_id=dev, device_id_type=MESH
        )

    loads = [
        pltpu.make_async_copy(src, dst, ws.at[i])
        for i, (src, dst) in enumerate(
            ((w_new_hbm, w_raw.at[0]), (w_old_hbm, w_raw.at[1]), (w_out_hbm, w_out))
        )
    ]
    for load in loads:
        load.start()

    barrier = pltpu.get_barrier_semaphore()
    for i in range(1, 16):
        pl.semaphore_signal(barrier, 1, device_id=xy_dev(peer(i // 4, i % 4)), device_id_type=MESH)
    for o in (1, 15, 2, 14):
        pl.semaphore_signal(barrier, 1, device_id=z_dev(o), device_id_type=MESH)
    for k in range(1, 8):
        pl.semaphore_signal(
            barrier, 1, device_id={"rep": lax.rem(rep + k, 8), "ep": ep}, device_id_type=MESH
        )
    half = pl.multiple_of(core * HALF, 128)
    other = pl.multiple_of((1 - core) * HALF, 128)
    mine = pl.ds(pl.multiple_of(zl * ROWS, ROWS), ROWS)
    square[...] = jnp.zeros((128, 128), F32)
    for i, table in enumerate((ro_t, rn_t, go_t, gn_t)):
        square[8 * i : 8 * i + 8, 0:ROWS] = table[...].astype(F32)
    meta_z[mine, :] = square[...].T[:ROWS, :]
    rz_old[mine, :] = rows_old[:, pl.ds(half, HALF)]
    rz_new[mine, :] = rows_new[:, pl.ds(pl.multiple_of(zh * 896 + core * 384, 128), WIN)]
    pl.semaphore_wait(barrier, 26)

    def z_copy(o, kind):
        offset = ZOFF[o]
        there = lax.rem(z + offset, 16) // 4
        if kind == 0:
            src, land = meta_z.at[mine, :], meta_z
        elif kind == 1:
            window = pl.ds(pl.multiple_of(there * 896 + core * 384, 128), WIN)
            src, land = rows_new.at[:, window], rz_new
        else:
            src, land = rows_old.at[:, pl.ds(half, HALF)], rz_old
        return remote(src, land.at[mine, :], zs.at[kind, o], zr.at[kind, o], z_dev(offset))

    def z_from(o, kind, buf):
        src = lax.rem(zl + 16 - ZOFF[o], 4)
        ref = buf.at[pl.ds(pl.multiple_of(src * ROWS, ROWS), ROWS), :]
        return remote(ref, ref, zs.at[kind, o], zr.at[kind, o], z_dev(ZOFF[o]))

    for kind in range(3):
        for o in range(3):
            z_copy(o, kind).start()
    for o in range(3):
        z_from(o, 0, meta_z).wait_recv()

    lane = iota((4 * ROWS, 128), 1)
    p_row, p_col = iota((4 * ROWS, 4 * ROWS), 0), iota((4 * ROWS, 4 * ROWS), 1)
    before = jnp.where((p_col < p_row) & (p_col >> 5 == p_row >> 5), 1.0, 0.0).astype(BF)
    qs = iota((16 * SLOTS, 128), 0)
    pick = jnp.where(by24(qs) * 4 + zl == iota((16 * SLOTS, 128), 1), 1.0, 0.0).astype(BF)
    in_q = qs - by24(qs) * 24
    slot_q = (in_q - by6(in_q) * 6).astype(F32)
    same_q = by6(in_q) == iota((16 * SLOTS, 128), 1) >> 5
    ql = iota((128, 16 * SLOTS), 1)
    in_l = ql - by24(ql) * 24
    slot_l = (in_l - by6(in_l) * 6).astype(F32)
    same_l = by6(in_l) == iota((128, 16 * SLOTS), 0) >> 5
    for b in range(2):
        named = jnp.zeros((4 * ROWS, 128), F32)
        gate = jnp.zeros((4 * ROWS, 128), F32)
        for k in range(TOPK):
            hit = meta_z[:, 8 * b + k : 8 * b + k + 1].astype(jnp.int32) == lane
            named = named + jnp.where(hit, 1.0, 0.0)
            gate = gate + jnp.where(hit, meta_z[:, 16 + 8 * b + k : 17 + 8 * b + k], 0.0)
        rank = dot(before, named.astype(BF))
        code = jnp.where(named > 0.5, rank, -1.0).astype(BF)
        disp[b] = jnp.where((dot_nt(pick, code) == slot_q) & same_q, 1.0, 0.0).astype(BF)
        chosen = (dot_nt(code, pick) == slot_l) & same_l
        high = gate.astype(BF)
        low = (gate - high.astype(F32)).astype(BF)
        comb[b, 0] = jnp.where(chosen, dot_nt(high, pick), 0.0).astype(BF)
        comb[b, 1] = jnp.where(chosen, dot_nt(low, pick), 0.0).astype(BF)

    def message_to(b, buf, land, dx, dy):
        d = peer(dx, dy)
        i = 4 * dx + dy
        return remote(buf.at[d], land.at[me], xs.at[b, i], xr.at[b, i], xy_dev(d))

    def message_from(b, land, dx, dy):
        d = peer(4 - dx, 4 - dy)
        i = 4 * dx + dy
        return d, remote(land.at[d], land.at[d], xs.at[b, i], xr.at[b, i], xy_dev(d))

    def put(buf, at, value, width):
        v = value.reshape(4, SLOTS, 2 * width)
        buf[at, 0:SLOTS, :] = v[:, :, :width].astype(BF)
        buf[at, SLOTS : 2 * SLOTS, :] = v[:, :, width:].astype(BF)

    def take(buf, g, h, width):
        v = buf[pl.ds(4 * g, 4), h * SLOTS : (h + 1) * SLOTS, :]
        return v.astype(F32).reshape(CH, width).astype(BF)

    def dispatch(b, rz, buf, land, width):
        for s in ORDER:
            g = lax.rem(x + s, 4)
            table = disp[b, pl.ds(pl.multiple_of(g * CH, 16), CH), :]
            put(buf, pl.ds(4 * g, 4), dot(table, rz[...]), width)
            for dy in (2, 1, 3, 0):
                if (s, dy) == (0, 0):
                    land[me] = buf[me]
                else:
                    message_to(b, buf, land, s, dy).start()

    for o in range(3):
        z_from(o, 1, rz_new).wait_recv()
    dispatch(1, rz_new, send_new, recv_new, WIN // 2)
    for o in range(3):
        z_from(o, 2, rz_old).wait_recv()
    dispatch(0, rz_old, send_old, recv_old, BLK)

    loads[0].wait()
    w_wide[...] = w_raw[0].astype(F32)
    pad = WIN - SLICE
    w_new[:, pl.ds(pl.multiple_of((1 - core) * SLICE, 64), pad), :] = jnp.zeros((2, pad, 1024), BF)
    top = pl.ds(pl.multiple_of(core * pad, 64), SLICE)
    for h in range(8):
        for g in range(2):
            col = (h // 2) * 256 + g * SLAB
            w_new[h % 2, top, col : col + SLAB] = w_wide[pl.ds(2 * h + g, SLICE, stride=16), :].astype(BF)

    def sx_copy(s):
        return remote(sx_send.at[s], sx_recv.at[s], sxs.at[s], sxr.at[s], sibling)

    def rs_copy(s, k):
        return remote(
            rs_send.at[s, lax.rem(zh + k, 4)], rs_recv.at[s, k - 1],
            rss.at[s, k - 1], rsr.at[s, k - 1], zh_dev(k),
        )

    def act_part(s):
        g = lax.rem(x + 4 - s, 4)
        for dy in (2, 1, 3, 0):
            if (s, dy) != (0, 0):
                message_from(1, recv_new, s, dy)[1].wait_recv()
        rows = [take(recv_new, g, h, WIN // 2) for h in range(2)]

        def part(c):
            return sum(dot(rows[h], w_new[c, h * (WIN // 2) : (h + 1) * (WIN // 2), :]) for h in range(2))

        sx_send[s] = part(1 - core).astype(BF)
        sx_copy(s).start()
        pn_own[s] = part(core)

    def act_send(s):
        sx_copy(s).wait_recv()
        for k in range(4):
            cols = slice(256 * k, 256 * (k + 1))
            rs_send[s, k] = (pn_own[s, :, cols] + sx_recv[s, :, cols].astype(F32)).astype(BF)
        for k in (2, 1, 3):
            rs_copy(s, k).start()

    def so_copy(b, s):
        return remote(so_send.at[b, s], so_recv.at[b, s], sos.at[b, s], sor.at[b, s], sibling)

    def down(b, s, act):
        gate = act[:, :SLAB]
        hidden = (gate / (1.0 + jnp.exp(-gate)) * act[:, SLAB:]).astype(BF)
        so_send[b, s] = dot(hidden, w_out[:, pl.ds(other, HALF)]).astype(BF)
        so_copy(b, s).start()
        po[b, s] = dot(hidden, w_out[:, pl.ds(half, HALF)])

    def back_to(b, dx, dy):
        d = peer(4 - dx, 4 - dy)
        i = 4 * dx + dy
        return remote(ret_send.at[b, d], ret_recv.at[b, me], rts.at[b, i], rtr.at[b, i], xy_dev(d))

    def back_from(b, dx, dy):
        d = peer(dx, dy)
        i = 4 * dx + dy
        return remote(ret_send.at[b, d], ret_recv.at[b, d], rts.at[b, i], rtr.at[b, i], xy_dev(d))

    def back(b, s):
        g = lax.rem(x + 4 - s, 4)
        so_copy(b, s).wait_recv()
        put(ret_send.at[b], pl.ds(4 * g, 4), po[b, s] + so_recv[b, s].astype(F32), BLK)
        for dy in (2, 1, 3, 0):
            if (s, dy) == (0, 0):
                ret_recv[b, me] = ret_send[b, me]
            else:
                back_to(b, s, dy).start()

    for n in range(5):
        if n < 4:
            act_part(ORDER[n])
        if n >= 1:
            act_send(ORDER[n - 1])

    def fwd_copy(s, dy):
        d = peer(4 - s, 4 - dy)
        i = 4 * s + dy
        return remote(recv_old.at[d], sib_old.at[d], fs.at[i], fr.at[i], sibling)

    def forward(s):
        for dy in (2, 1, 3, 0):
            if (s, dy) != (0, 0):
                message_from(0, recv_old, s, dy)[1].wait_recv()
            fwd_copy(s, dy).start()

    def act_old(s):
        g = lax.rem(x + 4 - s, 4)
        act = jnp.zeros((CH, 2 * SLAB), F32)
        for h in range(2):
            at = pl.ds(pl.multiple_of(half + h * BLK, 128), BLK)
            act += dot(take(recv_old, g, h, BLK), w_old[at, :])
        for dy in range(4):
            fwd_copy(s, dy).wait_recv()
        for h in range(2):
            at = pl.ds(pl.multiple_of(other + h * BLK, 128), BLK)
            act += dot(take(sib_old, g, h, BLK), w_old[at, :])
        down(0, s, act)

    loads[1].wait()
    w_wide[...] = w_raw[1].astype(F32)
    for g in range(2):
        w_old[:, g * SLAB : (g + 1) * SLAB] = w_wide[pl.ds(g, D, stride=2), :].astype(BF)
    loads[2].wait()

    for n in range(6):
        if n < 4:
            forward(ORDER[n])
        if 1 <= n < 5:
            act_old(ORDER[n - 1])
        if n >= 2:
            back(0, ORDER[n - 2])

    def act_new(s):
        act = rs_send[s, zh].astype(F32)
        for k in range(1, 4):
            rs_copy(s, k).wait_recv()
            act += rs_recv[s, k - 1].astype(F32)
        down(1, s, act)

    for n in range(5):
        if n < 4:
            act_new(ORDER[n])
        if n >= 1:
            back(1, ORDER[n - 1])

    def z1_copy(b, o):
        at = pl.ds(pl.multiple_of(lax.rem(zl + ZOFF[o], 4) * ROWS, ROWS), ROWS)
        return remote(z1_send.at[b, at, :], z1_recv.at[b, o], z1s.at[b, o], z1r.at[b, o], z_dev(ZOFF[o]))

    def combine(b):
        for i in range(1, 16):
            back_from(b, i // 4, i % 4).wait_recv()
        for h in range(2):
            rows = ret_recv[b, :, h * SLOTS : (h + 1) * SLOTS, :]
            rows = rows.astype(F32).reshape(16 * SLOTS, BLK).astype(BF)
            total = dot(comb[b, 0], rows) + dot(comb[b, 1], rows)
            cols = slice(h * BLK, (h + 1) * BLK)
            z1_own[b, :, cols] = total
            z1_send[b, :, cols] = total.astype(BF)
        for o in range(3):
            z1_copy(b, o).start()

    def z2_copy(b, t):
        k, c = t // 2, t % 2
        return remote(
            z2_send.at[b, :, k * 896 + c * 384 : k * 896 + c * 384 + WIN], z2_recv.at[b, zh],
            z2s.at[b, t], z2r.at[b, zh], {"rep": (2 * core + k) * 2 + c, "ep": ep},
        )

    def is_self(t):
        return rep == (2 * core + t // 2) * 2 + t % 2

    def spread(b):
        total = z1_own[b, mine, :]
        for o in range(3):
            z1_copy(b, o).wait_recv()
            total += z1_recv[b, o].astype(F32)
        z2_send[b] = total.astype(BF)
        for t in range(4):
            k, c = t // 2, t % 2

            @pl.when(jnp.logical_not(is_self(t)))
            def _():
                z2_copy(b, t).start()

            @pl.when(is_self(t))
            def _():
                z2_recv[b, zh] = z2_send[b, :, k * 896 + c * 384 : k * 896 + c * 384 + WIN]

    def finish(b, out):
        for s in range(4):

            @pl.when(jnp.logical_not((zh == s) & (core == zh // 2)))
            def _():
                ref = z2_recv.at[b, s]
                remote(ref, ref, z2s.at[b, 0], z2r.at[b, s], sibling).wait_recv()

        total = sum(z2_recv[b, s].astype(F32) for s in range(4))
        out[...] = jnp.where(core == 0, total[:, :SLICE], total[:, WIN - SLICE :]).astype(BF)

    combine(0)
    spread(0)
    combine(1)
    finish(0, out_old)
    spread(1)
    finish(1, out_new)

    for o in range(3):
        for kind in range(3):
            z_copy(o, kind).wait_send()
        for b in range(2):
            z1_copy(b, o).wait_send()
    for s in range(4):
        sx_copy(s).wait_send()
        for k in range(1, 4):
            rs_copy(s, k).wait_send()
        for dy in range(4):
            fwd_copy(s, dy).wait_send()
        for b in range(2):
            so_copy(b, s).wait_send()
            for dy in range(4):
                if (s, dy) != (0, 0):
                    message_to(b, (send_old, send_new)[b], (recv_old, recv_new)[b], s, dy).wait_send()
                    back_to(b, s, dy).wait_send()
    for b in range(2):
        for t in range(4):

            @pl.when(jnp.logical_not(is_self(t)))
            def _():
                z2_copy(b, t).wait_send()


def body(rows_old, rows_new, routes_old, routes_new, gates_old, gates_new, w_in_old, w_in_new, w_out):
    w_old = w_in_old[0].reshape(2 * D, SLAB)
    w_new = w_in_new[0].reshape(SLICE, 2, 8, SLAB).transpose(0, 2, 1, 3).reshape(SLICE * 16, SLAB)
    vmem = pl.BlockSpec(memory_space=pltpu.VMEM)
    dma = pltpu.SemaphoreType.DMA
    out = jax.ShapeDtypeStruct((ROWS, SLICE), BF)
    return pl.pallas_call(
        kernel,
        out_shape=(out, out),
        in_specs=[vmem] * 6 + [pl.BlockSpec(memory_space=pl.ANY)] * 3,
        out_specs=(vmem, vmem),
        scratch_shapes=[
            pltpu.VMEM((2, 2 * D, SLAB), BF),
            pltpu.VMEM((2 * D, SLAB), F32),
            pltpu.VMEM((D, 2 * SLAB), BF),
            pltpu.VMEM((2, WIN, 1024), BF),
            pltpu.VMEM((SLAB, D), BF),
            pltpu.VMEM((128, 128), F32),
            pltpu.VMEM((4 * ROWS, 128), F32),
            pltpu.VMEM((4 * ROWS, HALF), BF),
            pltpu.VMEM((4 * ROWS, WIN), BF),
            pltpu.VMEM((2, 16 * SLOTS, 128), BF),
            pltpu.VMEM((2, 2, 128, 16 * SLOTS), BF),
            pltpu.VMEM((16, 2 * SLOTS, WIN // 2), BF),
            pltpu.VMEM((16, 2 * SLOTS, WIN // 2), BF),
            pltpu.VMEM((16, 2 * SLOTS, BLK), BF),
            pltpu.VMEM((16, 2 * SLOTS, BLK), BF),
            pltpu.VMEM((16, 2 * SLOTS, BLK), BF),
            pltpu.VMEM((4, CH, 1024), F32),
            pltpu.VMEM((4, CH, 1024), BF),
            pltpu.VMEM((4, CH, 1024), BF),
            pltpu.VMEM((4, 4, CH, 256), BF),
            pltpu.VMEM((4, 3, CH, 256), BF),
            pltpu.VMEM((2, 4, CH, HALF), F32),
            pltpu.VMEM((2, 4, CH, HALF), BF),
            pltpu.VMEM((2, 4, CH, HALF), BF),
            pltpu.VMEM((2, 16, 2 * SLOTS, BLK), BF),
            pltpu.VMEM((2, 16, 2 * SLOTS, BLK), BF),
            pltpu.VMEM((2, 4 * ROWS, HALF), F32),
            pltpu.VMEM((2, 4 * ROWS, HALF), BF),
            pltpu.VMEM((2, 3, ROWS, HALF), BF),
            pltpu.VMEM((2, ROWS, HALF), BF),
            pltpu.VMEM((2, 4, ROWS, WIN), BF),
            dma((3,)),
            dma((3, 3)), dma((3, 3)),
            dma((2, 16)), dma((2, 16)),
            dma((16,)), dma((16,)),
            dma((4,)), dma((4,)),
            dma((4, 3)), dma((4, 3)),
            dma((2, 4)), dma((2, 4)),
            dma((2, 16)), dma((2, 16)),
            dma((2, 3)), dma((2, 3)),
            dma((2, 4)), dma((2, 4)),
        ],
        compiler_params=pltpu.CompilerParams(
            collective_id=0, has_side_effects=True, vmem_limit_bytes=60 * 1024 * 1024
        ),
    )(routes_old.T, routes_new.T, gates_old.T, gates_new.T, rows_old, rows_new, w_old, w_new, w_out[0])


def solution(mesh):
    return jax.shard_map(
        body,
        mesh=mesh,
        in_specs=(
            P("ep", None),
            P("ep", None),
            P("ep", None),
            P("ep", None),
            P("ep", None),
            P("ep", None),
            P("ep", None, None, "rep"),
            P("ep", "rep", None, None),
            P("ep", "rep", None),
        ),
        out_specs=(P("ep", "rep"), P("ep", "rep")),
        check_vma=False,
    )
```

```python
import functools

import jax
import jax.numpy as jnp
from jax import lax
from jax.experimental import pallas as pl
from jax.experimental.pallas import tpu as pltpu
from jax.sharding import PartitionSpec as P

BF = jnp.bfloat16
F32 = jnp.float32
MESH = pl.DeviceIdType.MESH

D = 3584
HALF = D // 2
BLK = HALF // 2
WIN = 512
SLICE = 448
SLAB = 128
TOPK = 8
ROWS = 32
CAP = 6
SLOTS = 4 * CAP
CH = 4 * SLOTS
FAR = (2, 1, 3, 0)
PLACE = tuple((dx, (total - dx) % 4) for total in FAR for dx in FAR)
PART_A, PART_B = 512, 384
PARTS = ((0, PART_A), (2 * PART_A, PART_B))
ZOFF = (1, 15, 2)


def dot(a, b):
    return lax.dot_general(a, b, (((1,), (0,)), ((), ())), preferred_element_type=F32)


def dot_nt(a, b):
    return lax.dot_general(a, b, (((1,), (1,)), ((), ())), preferred_element_type=F32)


def iota(shape, dim):
    return lax.broadcasted_iota(jnp.int32, shape, dim)


def by24(q):
    return (q * 2731) >> 16


def by6(q):
    return (q * 10923) >> 16


def far(m):
    return jnp.where(m == 0, 2, jnp.where(m == 3, 0, 2 * m - 1))


def kernel(
    ro_t, rn_t, go_t, gn_t, rows_old, rows_new, w_old_hbm, w_new_hbm, w_out_hbm,
    out_old, out_new,
    w_raw, w_wide, w_old, w_new, w_out, square, meta_z, rz_old, rz_new, disp, comb,
    send_new, recv_new, send_old, recv_old, sib_old,
    pn, sx_send, sx_recv, rf_send, rf_recv, rn_send, rn_recv,
    po, so_send, so_recv, ra_send, ra_recv, rb_send, rb_recv,
    z1_own, z1_send, z1_recv, z2_send, z2_recv,
    ws, zs, zr, xs, xr, fs, fr, sxs, sxr, rfs, rfr, rns, rnr, sos, sor, rts, rtr, z1s, z1r, z2s, z2r,
):
    ep = lax.axis_index("ep")
    rep = lax.axis_index("rep")
    core, zh = lax.rem(rep, 2), rep // 2
    zl, me = lax.rem(ep, 4), ep // 4
    x, y = me // 4, lax.rem(me, 4)
    z = zh * 4 + zl

    def z_dev(offset):
        t = lax.rem(z + offset, 16)
        return {"rep": (t // 4) * 2 + core, "ep": me * 4 + lax.rem(t, 4)}

    def to_dev(r):
        dx, dy = PLACE[r]
        return {"rep": rep, "ep": (lax.rem(x + dx, 4) * 4 + lax.rem(y + dy, 4)) * 4 + zl}

    def from_dev(r):
        dx, dy = PLACE[r]
        return {"rep": rep, "ep": (lax.rem(x + 4 - dx, 4) * 4 + lax.rem(y + 4 - dy, 4)) * 4 + zl}

    def zh_dev(k):
        return {"rep": lax.rem(zh + k, 4) * 2 + core, "ep": ep}

    sibling = {"rep": zh * 2 + (1 - core), "ep": ep}

    def remote(src, dst, ss, rs, dev):
        return pltpu.make_async_remote_copy(
            src_ref=src, dst_ref=dst, send_sem=ss, recv_sem=rs, device_id=dev, device_id_type=MESH
        )

    loads = [
        pltpu.make_async_copy(src, dst, ws.at[i])
        for i, (src, dst) in enumerate(
            ((w_new_hbm, w_raw.at[0]), (w_old_hbm, w_raw.at[1]), (w_out_hbm, w_out))
        )
    ]
    for load in loads:
        load.start()

    barrier = pltpu.get_barrier_semaphore()
    for r in range(15):
        pl.semaphore_signal(barrier, 1, device_id=to_dev(r), device_id_type=MESH)
    for o in (1, 15, 2, 14):
        pl.semaphore_signal(barrier, 1, device_id=z_dev(o), device_id_type=MESH)
    for k in range(1, 8):
        pl.semaphore_signal(
            barrier, 1, device_id={"rep": lax.rem(rep + k, 8), "ep": ep}, device_id_type=MESH
        )
    half = pl.multiple_of(core * HALF, 128)
    other = pl.multiple_of((1 - core) * HALF, 128)
    mine = pl.ds(pl.multiple_of(zl * ROWS, ROWS), ROWS)
    square[...] = jnp.zeros((128, 128), F32)
    for i, table in enumerate((ro_t, rn_t, go_t, gn_t)):
        square[8 * i : 8 * i + 8, 0:ROWS] = table[...].astype(F32)
    meta_z[mine, :] = square[...].T[:ROWS, :]
    rz_old[mine, :] = rows_old[:, pl.ds(half, HALF)]
    rz_new[mine, :] = rows_new[:, pl.ds(pl.multiple_of(zh * 896 + core * 384, 128), WIN)]
    pl.semaphore_wait(barrier, 26)

    def z_copy(o, kind):
        offset = ZOFF[o]
        there = lax.rem(z + offset, 16) // 4
        if kind == 0:
            src, land = meta_z.at[mine, :], meta_z
        elif kind == 1:
            window = pl.ds(pl.multiple_of(there * 896 + core * 384, 128), WIN)
            src, land = rows_new.at[:, window], rz_new
        else:
            src, land = rows_old.at[:, pl.ds(half, HALF)], rz_old
        return remote(src, land.at[mine, :], zs.at[kind, o], zr.at[kind, o], z_dev(offset))

    def z_from(o, kind, buf):
        src = lax.rem(zl + 16 - ZOFF[o], 4)
        ref = buf.at[pl.ds(pl.multiple_of(src * ROWS, ROWS), ROWS), :]
        return remote(ref, ref, zs.at[kind, o], zr.at[kind, o], z_dev(ZOFF[o]))

    for kind in range(3):
        for o in range(3):
            z_copy(o, kind).start()
    for o in range(3):
        z_from(o, 0, meta_z).wait_recv()

    lane = iota((4 * ROWS, 128), 1)
    p_row, p_col = iota((4 * ROWS, 4 * ROWS), 0), iota((4 * ROWS, 4 * ROWS), 1)
    before = jnp.where((p_col < p_row) & (p_col >> 5 == p_row >> 5), 1.0, 0.0).astype(BF)
    qs = iota((16 * SLOTS, 128), 0)
    rq = by24(qs)
    dx = far(rq & 3)
    dy = (far(rq >> 2) - dx) & 3
    expert = (((x + dx) & 3) * 4 + ((y + dy) & 3)) * 4 + zl
    pick = jnp.where(expert == iota((16 * SLOTS, 128), 1), 1.0, 0.0).astype(BF)
    in_q = qs - by24(qs) * 24
    slot_q = (in_q - by6(in_q) * 6).astype(F32)
    same_q = by6(in_q) == iota((16 * SLOTS, 128), 1) >> 5
    ql = iota((128, 16 * SLOTS), 1)
    in_l = ql - by24(ql) * 24
    slot_l = (in_l - by6(in_l) * 6).astype(F32)
    same_l = by6(in_l) == iota((128, 16 * SLOTS), 0) >> 5
    for b in range(2):
        named = jnp.zeros((4 * ROWS, 128), F32)
        gate = jnp.zeros((4 * ROWS, 128), F32)
        for k in range(TOPK):
            hit = meta_z[:, 8 * b + k : 8 * b + k + 1].astype(jnp.int32) == lane
            named = named + jnp.where(hit, 1.0, 0.0)
            gate = gate + jnp.where(hit, meta_z[:, 16 + 8 * b + k : 17 + 8 * b + k], 0.0)
        rank = dot(before, named.astype(BF))
        code = jnp.where(named > 0.5, rank, -1.0).astype(BF)
        disp[b] = jnp.where((dot_nt(pick, code) == slot_q) & same_q, 1.0, 0.0).astype(BF)
        chosen = (dot_nt(code, pick) == slot_l) & same_l
        high = gate.astype(BF)
        low = (gate - high.astype(F32)).astype(BF)
        comb[b, 0] = jnp.where(chosen, dot_nt(high, pick), 0.0).astype(BF)
        comb[b, 1] = jnp.where(chosen, dot_nt(low, pick), 0.0).astype(BF)

    def message(b, buf, land, r):
        return remote(buf.at[r], land.at[r], xs.at[b, r], xr.at[b, r], to_dev(r))

    def put(buf, n, value, width):
        v = value.reshape(4, SLOTS, 2 * width)
        buf[4 * n : 4 * n + 4, 0:SLOTS, :] = v[:, :, :width].astype(BF)
        buf[4 * n : 4 * n + 4, SLOTS : 2 * SLOTS, :] = v[:, :, width:].astype(BF)

    def take(buf, n, h, width):
        v = buf[4 * n : 4 * n + 4, h * SLOTS : (h + 1) * SLOTS, :]
        return v.astype(F32).reshape(CH, width).astype(BF)

    def dispatch(b, rz, buf, land, width):
        for n in range(4):
            put(buf, n, dot(disp[b, n * CH : (n + 1) * CH, :], rz[...]), width)
            for r in range(4 * n, 4 * n + 4):
                if r < 15:
                    message(b, buf, land, r).start()
                else:
                    land[15] = buf[15]

    for o in range(3):
        z_from(o, 1, rz_new).wait_recv()
    dispatch(1, rz_new, send_new, recv_new, WIN // 2)
    for o in range(3):
        z_from(o, 2, rz_old).wait_recv()
    dispatch(0, rz_old, send_old, recv_old, BLK)

    loads[0].wait()
    w_wide[...] = w_raw[0].astype(F32)
    pad = WIN - SLICE
    w_new[:, pl.ds(pl.multiple_of((1 - core) * SLICE, 64), pad), :] = jnp.zeros((2, pad, 1024), BF)
    top = pl.ds(pl.multiple_of(core * pad, 64), SLICE)
    for h in range(8):
        for g in range(2):
            col = pl.multiple_of(lax.rem(h // 2 + 4 - zh, 4) * 256 + g * SLAB, SLAB)
            w_new[h % 2, top, pl.ds(col, SLAB)] = w_wide[pl.ds(2 * h + g, SLICE, stride=16), :].astype(BF)

    def sx_copy(n):
        return remote(sx_send.at[n], sx_recv.at[n], sxs.at[n], sxr.at[n], sibling)

    def rf_copy(n, i):
        return remote(rf_send.at[n, i], rf_recv.at[n, i], rfs.at[n, i], rfr.at[n, i], zh_dev(1 + 2 * i))

    def rn_copy(n, i):
        return remote(rn_send.at[n, i], rn_recv.at[n, i], rns.at[n, i], rnr.at[n, i], zh_dev(1 + 2 * i))

    def act_part(n):
        for r in range(4 * n, min(4 * n + 4, 15)):
            message(1, send_new, recv_new, r).wait_recv()
        rows = [take(recv_new, n, h, WIN // 2) for h in range(2)]

        def part(c):
            return sum(dot(rows[h], w_new[c, h * (WIN // 2) : (h + 1) * (WIN // 2), :]) for h in range(2))

        sx_send[n] = part(1 - core).astype(BF)
        sx_copy(n).start()
        pn[n] = part(core)

    def act_far(n):
        sx_copy(n).wait_recv()
        total = pn[n] + sx_recv[n].astype(F32)
        for i in range(2):
            rf_send[n, i] = total[i * CH // 2 : (i + 1) * CH // 2, 512:768].astype(BF)
            rf_copy(n, i).start()
        pn[n] = total

    def act_near(n):
        for i in range(2):
            rf_copy(n, i).wait_recv()
            cols = slice(256 + 512 * i, 512 + 512 * i)
            own, more = slice((1 - i) * CH // 2, (2 - i) * CH // 2), slice(i * CH // 2, (i + 1) * CH // 2)
            rn_send[n, i, own, :] = pn[n, own, cols].astype(BF)
            rn_send[n, i, more, :] = (pn[n, more, cols] + rf_recv[n, i].astype(F32)).astype(BF)
            rn_copy(n, i).start()

    def so_copy(b, n):
        return remote(so_send.at[b, n], so_recv.at[b, n], sos.at[b, n], sor.at[b, n], sibling)

    def down(b, n, act):
        gate = act[:, :SLAB]
        hidden = (gate / (1.0 + jnp.exp(-gate)) * act[:, SLAB:]).astype(BF)
        so_send[b, n] = dot(hidden, w_out[:, pl.ds(other, HALF)]).astype(BF)
        so_copy(b, n).start()
        po[b, n] = dot(hidden, w_out[:, pl.ds(half, HALF)])

    def back(b, part, r):
        src, land = ((ra_send, ra_recv), (rb_send, rb_recv))[part]
        return remote(src.at[b, r], land.at[b, r], rts.at[b, part, r], rtr.at[b, part, r], from_dev(r))

    def chip_sum(b, n):
        so_copy(b, n).wait_recv()
        total = po[b, n] + so_recv[b, n].astype(F32)
        put(ra_send.at[b], n, total[:, : 2 * PART_A], PART_A)
        put(rb_send.at[b], n, total[:, 2 * PART_A :], PART_B)

    def send_back(b, part, n):
        for r in range(4 * n, 4 * n + 4):
            if r < 15:
                back(b, part, r).start()
            elif part == 0:
                ra_recv[b, 15] = ra_send[b, 15]
            else:
                rb_recv[b, 15] = rb_send[b, 15]

    for n in range(6):
        if n < 4:
            act_part(n)
        if 1 <= n < 5:
            act_far(n - 1)
        if n >= 2:
            act_near(n - 2)

    def fwd_copy(r):
        return remote(recv_old.at[r], sib_old.at[r], fs.at[r], fr.at[r], sibling)

    def forward(n):
        for r in range(4 * n, 4 * n + 4):
            if r < 15:
                message(0, send_old, recv_old, r).wait_recv()
            fwd_copy(r).start()

    def act_old(n):
        act = jnp.zeros((CH, 2 * SLAB), F32)
        for h in range(2):
            at = pl.ds(pl.multiple_of(half + h * BLK, 128), BLK)
            act += dot(take(recv_old, n, h, BLK), w_old[at, :])
        for r in range(4 * n, 4 * n + 4):
            fwd_copy(r).wait_recv()
        for h in range(2):
            at = pl.ds(pl.multiple_of(other + h * BLK, 128), BLK)
            act += dot(take(sib_old, n, h, BLK), w_old[at, :])
        down(0, n, act)

    loads[1].wait()
    w_wide[...] = w_raw[1].astype(F32)
    for g in range(2):
        w_old[:, g * SLAB : (g + 1) * SLAB] = w_wide[pl.ds(g, D, stride=2), :].astype(BF)
    loads[2].wait()

    for n in range(6):
        if n < 4:
            forward(n)
        if 1 <= n < 5:
            act_old(n - 1)
        if n >= 2:
            chip_sum(0, n - 2)
            send_back(0, 0, n - 2)
            send_back(0, 1, n - 2)

    def act_new(n):
        act = pn[n, :, 0:256]
        for i in range(2):
            rn_copy(n, i).wait_recv()
            act += rn_recv[n, i].astype(F32)
        down(1, n, act)

    for n in range(6):
        if n < 4:
            act_new(n)
        if 1 <= n < 5:
            chip_sum(1, n - 1)
            send_back(1, 0, n - 1)
        if n >= 2:
            send_back(1, 1, n - 2)

    def z1_copy(b, part, o):
        at = pl.ds(pl.multiple_of(lax.rem(zl + ZOFF[o], 4) * ROWS, ROWS), ROWS)
        col, width = PARTS[part]
        cols = slice(col, col + 2 * width)
        return remote(
            z1_send.at[b, at, cols], z1_recv.at[b, o, :, cols],
            z1s.at[b, part, o], z1r.at[b, part, o], z_dev(ZOFF[o]),
        )

    def combine(b, part):
        for r in range(15):
            back(b, part, r).wait_recv()
        col, width = PARTS[part]
        for h in range(2):
            rows = (ra_recv, rb_recv)[part][b, :, h * SLOTS : (h + 1) * SLOTS, :]
            rows = rows.astype(F32).reshape(16 * SLOTS, width).astype(BF)
            total = dot(comb[b, 0], rows) + dot(comb[b, 1], rows)
            cols = slice(col + h * width, col + (h + 1) * width)
            z1_own[b, :, cols] = total
            z1_send[b, :, cols] = total.astype(BF)
        for o in range(3):
            z1_copy(b, part, o).start()

    def z2_copy(b, t):
        k, c = t // 2, t % 2
        return remote(
            z2_send.at[b, :, k * 896 + c * 384 : k * 896 + c * 384 + WIN], z2_recv.at[b, zh],
            z2s.at[b, t], z2r.at[b, zh], {"rep": (2 * core + k) * 2 + c, "ep": ep},
        )

    def is_self(t):
        return rep == (2 * core + t // 2) * 2 + t % 2

    def spread(b, part):
        col, width = PARTS[part]
        cols = slice(col, col + 2 * width)
        total = z1_own[b, mine, cols]
        for o in range(3):
            z1_copy(b, part, o).wait_recv()
            total += z1_recv[b, o, :, cols].astype(F32)
        z2_send[b, :, cols] = total.astype(BF)
        for t in (2 * part, 2 * part + 1):
            k, c = t // 2, t % 2

            @pl.when(jnp.logical_not(is_self(t)))
            def _():
                z2_copy(b, t).start()

            @pl.when(is_self(t))
            def _():
                z2_recv[b, zh] = z2_send[b, :, k * 896 + c * 384 : k * 896 + c * 384 + WIN]

    def finish(b, out):
        for s in range(4):

            @pl.when(jnp.logical_not((zh == s) & (core == zh // 2)))
            def _():
                ref = z2_recv.at[b, s]
                remote(ref, ref, z2s.at[b, 0], z2r.at[b, s], sibling).wait_recv()

        total = sum(z2_recv[b, s].astype(F32) for s in range(4))
        out[...] = jnp.where(core == 0, total[:, :SLICE], total[:, WIN - SLICE :]).astype(BF)

    combine(0, 0)
    combine(0, 1)
    spread(0, 0)
    spread(0, 1)
    finish(0, out_old)
    combine(1, 0)
    spread(1, 0)
    combine(1, 1)
    spread(1, 1)
    finish(1, out_new)

    for o in range(3):
        for kind in range(3):
            z_copy(o, kind).wait_send()
        for b in range(2):
            for part in range(2):
                z1_copy(b, part, o).wait_send()
    for n in range(4):
        sx_copy(n).wait_send()
        for i in range(2):
            rf_copy(n, i).wait_send()
            rn_copy(n, i).wait_send()
        for b in range(2):
            so_copy(b, n).wait_send()
    for r in range(16):
        fwd_copy(r).wait_send()
    for r in range(15):
        message(0, send_old, recv_old, r).wait_send()
        message(1, send_new, recv_new, r).wait_send()
        for b in range(2):
            for part in range(2):
                back(b, part, r).wait_send()
    for b in range(2):
        for t in range(4):

            @pl.when(jnp.logical_not(is_self(t)))
            def _():
                z2_copy(b, t).wait_send()


def body(rows_old, rows_new, routes_old, routes_new, gates_old, gates_new, w_in_old, w_in_new, w_out):
    w_old = w_in_old[0].reshape(2 * D, SLAB)
    w_new = w_in_new[0].reshape(SLICE, 2, 8, SLAB).transpose(0, 2, 1, 3).reshape(SLICE * 16, SLAB)
    vmem = pl.BlockSpec(memory_space=pltpu.VMEM)
    dma = pltpu.SemaphoreType.DMA
    out = jax.ShapeDtypeStruct((ROWS, SLICE), BF)
    return pl.pallas_call(
        kernel,
        out_shape=(out, out),
        in_specs=[vmem] * 6 + [pl.BlockSpec(memory_space=pl.ANY)] * 3,
        out_specs=(vmem, vmem),
        scratch_shapes=[
            pltpu.VMEM((2, 2 * D, SLAB), BF),
            pltpu.VMEM((2 * D, SLAB), F32),
            pltpu.VMEM((D, 2 * SLAB), BF),
            pltpu.VMEM((2, WIN, 1024), BF),
            pltpu.VMEM((SLAB, D), BF),
            pltpu.VMEM((128, 128), F32),
            pltpu.VMEM((4 * ROWS, 128), F32),
            pltpu.VMEM((4 * ROWS, HALF), BF),
            pltpu.VMEM((4 * ROWS, WIN), BF),
            pltpu.VMEM((2, 16 * SLOTS, 128), BF),
            pltpu.VMEM((2, 2, 128, 16 * SLOTS), BF),
            pltpu.VMEM((16, 2 * SLOTS, WIN // 2), BF),
            pltpu.VMEM((16, 2 * SLOTS, WIN // 2), BF),
            pltpu.VMEM((16, 2 * SLOTS, BLK), BF),
            pltpu.VMEM((16, 2 * SLOTS, BLK), BF),
            pltpu.VMEM((16, 2 * SLOTS, BLK), BF),
            pltpu.VMEM((4, CH, 1024), F32),
            pltpu.VMEM((4, CH, 1024), BF),
            pltpu.VMEM((4, CH, 1024), BF),
            pltpu.VMEM((4, 2, CH // 2, 256), BF),
            pltpu.VMEM((4, 2, CH // 2, 256), BF),
            pltpu.VMEM((4, 2, CH, 256), BF),
            pltpu.VMEM((4, 2, CH, 256), BF),
            pltpu.VMEM((2, 4, CH, HALF), F32),
            pltpu.VMEM((2, 4, CH, HALF), BF),
            pltpu.VMEM((2, 4, CH, HALF), BF),
            pltpu.VMEM((2, 16, 2 * SLOTS, PART_A), BF),
            pltpu.VMEM((2, 16, 2 * SLOTS, PART_A), BF),
            pltpu.VMEM((2, 16, 2 * SLOTS, PART_B), BF),
            pltpu.VMEM((2, 16, 2 * SLOTS, PART_B), BF),
            pltpu.VMEM((2, 4 * ROWS, HALF), F32),
            pltpu.VMEM((2, 4 * ROWS, HALF), BF),
            pltpu.VMEM((2, 3, ROWS, HALF), BF),
            pltpu.VMEM((2, ROWS, HALF), BF),
            pltpu.VMEM((2, 4, ROWS, WIN), BF),
            dma((3,)),
            dma((3, 3)), dma((3, 3)),
            dma((2, 16)), dma((2, 16)),
            dma((16,)), dma((16,)),
            dma((4,)), dma((4,)),
            dma((4, 2)), dma((4, 2)),
            dma((4, 2)), dma((4, 2)),
            dma((2, 4)), dma((2, 4)),
            dma((2, 2, 16)), dma((2, 2, 16)),
            dma((2, 2, 3)), dma((2, 2, 3)),
            dma((2, 4)), dma((2, 4)),
        ],
        compiler_params=pltpu.CompilerParams(
            collective_id=0, has_side_effects=True, vmem_limit_bytes=60 * 1024 * 1024
        ),
    )(routes_old.T, routes_new.T, gates_old.T, gates_new.T, rows_old, rows_new, w_old, w_new, w_out[0])


def solution(mesh):
    return jax.shard_map(
        body,
        mesh=mesh,
        in_specs=(
            P("ep", None),
            P("ep", None),
            P("ep", None),
            P("ep", None),
            P("ep", None),
            P("ep", None),
            P("ep", None, None, "rep"),
            P("ep", "rep", None, None),
            P("ep", "rep", None),
        ),
        out_specs=(P("ep", "rep"), P("ep", "rep")),
        check_vma=False,
    )
```

```python
import functools

import jax
import jax.numpy as jnp
from jax import lax
from jax.experimental import pallas as pl
from jax.experimental.pallas import tpu as pltpu
from jax.sharding import PartitionSpec as P

BF = jnp.bfloat16
F32 = jnp.float32
MESH = pl.DeviceIdType.MESH

D = 3584
HALF = D // 2
BLK = HALF // 2
WIN = 512
SLICE = 448
SLAB = 128
TOPK = 8
ROWS = 32
CAP = 6
SLOTS = 4 * CAP
CH = 4 * SLOTS
FAR = (2, 1, 3, 0)
PLACE = tuple((dx, dy) for dx in FAR for dy in FAR)
PART_A, PART_B = 512, 384
PARTS = ((0, PART_A), (2 * PART_A, PART_B))


def dot(a, b):
    return lax.dot_general(a, b, (((1,), (0,)), ((), ())), preferred_element_type=F32)


def dot_nt(a, b):
    return lax.dot_general(a, b, (((1,), (1,)), ((), ())), preferred_element_type=F32)


def iota(shape, dim):
    return lax.broadcasted_iota(jnp.int32, shape, dim)


def by24(q):
    return (q * 2731) >> 16


def by6(q):
    return (q * 10923) >> 16


def far(m):
    return jnp.where(m == 0, 2, jnp.where(m == 3, 0, 2 * m - 1))


def kernel(
    ro_t, rn_t, go_t, gn_t, rows_old, rows_new, w_old_hbm, w_new_hbm, w_out_hbm,
    out_old, out_new,
    tab_i, tab_f, result,
    w_raw, w_wide, w_old, w_new, w_out, square, meta_z, rz_old, rz_new, disp, comb,
    send_new, recv_new, send_old, recv_old, sib_old,
    pn, sx_send, sx_recv, rf_send, rf_recv, rn_send, rn_recv,
    po, so_send, so_recv, ra_send, ra_recv, rb_send, rb_recv,
    z1_own, z1_send, z1_recv, z2_send, z2_recv,
    ins, ws, zs, zr, xs, xr, fs, fr, sxs, sxr, rfs, rfr, rns, rnr, sos, sor, rts, rtr, z1s, z1r, z2s, z2r,
):
    ep = lax.axis_index("ep")
    rep = lax.axis_index("rep")
    core, zh = lax.rem(rep, 2), rep // 2
    zl, me = lax.rem(ep, 4), ep // 4
    x, y = me // 4, lax.rem(me, 4)
    z = zh * 4 + zl
    zoff = (1, 15, 2 + 12 * core)

    def z_dev(offset):
        t = lax.rem(z + offset, 16)
        return {"rep": (t // 4) * 2 + core, "ep": me * 4 + lax.rem(t, 4)}

    def to_dev(r):
        dx, dy = PLACE[r]
        return {"rep": rep, "ep": (lax.rem(x + dx, 4) * 4 + lax.rem(y + dy, 4)) * 4 + zl}

    def from_dev(r):
        dx, dy = PLACE[r]
        return {"rep": rep, "ep": (lax.rem(x + 4 - dx, 4) * 4 + lax.rem(y + 4 - dy, 4)) * 4 + zl}

    def zh_dev(k):
        return {"rep": lax.rem(zh + k, 4) * 2 + core, "ep": ep}

    sibling = {"rep": zh * 2 + (1 - core), "ep": ep}

    def remote(src, dst, ss, rs, dev):
        return pltpu.make_async_remote_copy(
            src_ref=src, dst_ref=dst, send_sem=ss, recv_sem=rs, device_id=dev, device_id_type=MESH
        )

    half = pl.multiple_of(core * HALF, 128)
    other = pl.multiple_of((1 - core) * HALF, 128)
    mine = pl.ds(pl.multiple_of(zl * ROWS, ROWS), ROWS)
    window = pl.ds(pl.multiple_of(zh * 896 + core * 384, 128), WIN)
    inputs = [
        pltpu.make_async_copy(src, dst, ins.at[i])
        for i, (src, dst) in enumerate(
            (
                (ro_t, tab_i.at[0]), (rn_t, tab_i.at[1]), (go_t, tab_f.at[0]), (gn_t, tab_f.at[1]),
                (rows_new.at[:, window], rz_new.at[mine, :]),
                (rows_old.at[:, pl.ds(half, HALF)], rz_old.at[mine, :]),
            )
        )
    ]
    for copy in inputs:
        copy.start()

    barrier = pltpu.get_barrier_semaphore()
    for r in range(15):
        pl.semaphore_signal(barrier, 1, device_id=to_dev(r), device_id_type=MESH)
    for o in (1, 15, 2, 14):
        pl.semaphore_signal(barrier, 1, device_id=z_dev(o), device_id_type=MESH)
    for k in range(1, 8):
        pl.semaphore_signal(
            barrier, 1, device_id={"rep": lax.rem(rep + k, 8), "ep": ep}, device_id_type=MESH
        )
    loads = [
        pltpu.make_async_copy(src, dst, ws.at[i])
        for i, (src, dst) in enumerate(
            ((w_new_hbm, w_raw.at[0]), (w_old_hbm, w_raw.at[1]), (w_out_hbm, w_out))
        )
    ]
    for load in loads:
        load.start()

    square[...] = jnp.zeros((128, 128), F32)
    for copy in inputs[:4]:
        copy.wait()
    for i, table in enumerate((tab_i.at[0], tab_i.at[1], tab_f.at[0], tab_f.at[1])):
        square[8 * i : 8 * i + 8, 0:ROWS] = table[...].astype(F32)
    meta_z[mine, :] = square[...].T[:ROWS, :]

    lane = iota((4 * ROWS, 128), 1)
    p_row, p_col = iota((4 * ROWS, 4 * ROWS), 0), iota((4 * ROWS, 4 * ROWS), 1)
    before = jnp.where((p_col < p_row) & (p_col >> 5 == p_row >> 5), 1.0, 0.0).astype(BF)
    qs = iota((16 * SLOTS, 128), 0)
    rq = by24(qs)
    dx = far(rq >> 2)
    dy = far(rq & 3)
    expert = (((x + dx) & 3) * 4 + ((y + dy) & 3)) * 4 + zl
    pick = jnp.where(expert == iota((16 * SLOTS, 128), 1), 1.0, 0.0).astype(BF)
    in_q = qs - by24(qs) * 24
    slot_q = (in_q - by6(in_q) * 6).astype(F32)
    same_q = by6(in_q) == iota((16 * SLOTS, 128), 1) >> 5
    ql = iota((128, 16 * SLOTS), 1)
    in_l = ql - by24(ql) * 24
    slot_l = (in_l - by6(in_l) * 6).astype(F32)
    same_l = by6(in_l) == iota((128, 16 * SLOTS), 0) >> 5
    pl.semaphore_wait(barrier, 26)

    def z_copy(o, kind):
        offset = zoff[o]
        there = lax.rem(z + offset, 16) // 4
        if kind == 0:
            src, land = meta_z.at[mine, :], meta_z
        elif kind == 1:
            theirs = pl.ds(pl.multiple_of(there * 896 + core * 384, 128), WIN)
            src, land = rows_new.at[:, theirs], rz_new
        else:
            src, land = rows_old.at[:, pl.ds(half, HALF)], rz_old
        return remote(src, land.at[mine, :], zs.at[kind, o], zr.at[kind, o], z_dev(offset))

    def z_from(o, kind, buf):
        src = lax.rem(zl + 16 - zoff[o], 4)
        ref = buf.at[pl.ds(pl.multiple_of(src * ROWS, ROWS), ROWS), :]
        return remote(ref, ref, zs.at[kind, o], zr.at[kind, o], z_dev(zoff[o]))

    for kind in range(3):
        for o in range(3):
            z_copy(o, kind).start()
    for o in range(3):
        z_from(o, 0, meta_z).wait_recv()

    def tables(b):
        named = jnp.zeros((4 * ROWS, 128), F32)
        gate = jnp.zeros((4 * ROWS, 128), F32)
        for k in range(TOPK):
            hit = meta_z[:, 8 * b + k : 8 * b + k + 1].astype(jnp.int32) == lane
            named = named + jnp.where(hit, 1.0, 0.0)
            gate = gate + jnp.where(hit, meta_z[:, 16 + 8 * b + k : 17 + 8 * b + k], 0.0)
        rank = dot(before, named.astype(BF))
        code = jnp.where(named > 0.5, rank, -1.0).astype(BF)
        disp[b] = jnp.where((dot_nt(pick, code) == slot_q) & same_q, 1.0, 0.0).astype(BF)
        chosen = (dot_nt(code, pick) == slot_l) & same_l
        high = gate.astype(BF)
        low = (gate - high.astype(F32)).astype(BF)
        comb[b, 0] = jnp.where(chosen, dot_nt(high, pick), 0.0).astype(BF)
        comb[b, 1] = jnp.where(chosen, dot_nt(low, pick), 0.0).astype(BF)

    def message(b, buf, land, r):
        return remote(buf.at[r], land.at[r], xs.at[b, r], xr.at[b, r], to_dev(r))

    def put(buf, n, value, width):
        v = value.reshape(4, SLOTS, 2 * width)
        buf[4 * n : 4 * n + 4, 0:SLOTS, :] = v[:, :, :width].astype(BF)
        buf[4 * n : 4 * n + 4, SLOTS : 2 * SLOTS, :] = v[:, :, width:].astype(BF)

    def take(buf, n, h, width):
        v = buf[4 * n : 4 * n + 4, h * SLOTS : (h + 1) * SLOTS, :]
        return v.astype(F32).reshape(CH, width).astype(BF)

    def send_out(b, buf, land, n):
        for r in range(4 * n, 4 * n + 4):
            if r < 15:
                message(b, buf, land, r).start()
            else:
                land[15] = buf[15]

    def dispatch(b, rz, buf, land, width, ahead):
        for n in range(4):
            put(buf, n, dot(disp[b, n * CH : (n + 1) * CH, :], rz[...]), width)
            if n < ahead:
                send_out(b, buf, land, n)

    tables(1)
    for o in range(3):
        z_from(o, 1, rz_new).wait_recv()
    inputs[4].wait()
    dispatch(1, rz_new, send_new, recv_new, WIN // 2, 4)
    tables(0)
    for o in range(3):
        z_from(o, 2, rz_old).wait_recv()
    inputs[5].wait()
    dispatch(0, rz_old, send_old, recv_old, BLK, 2)

    loads[0].wait()
    w_wide[...] = w_raw[0].astype(F32)
    pad = WIN - SLICE
    w_new[:, pl.ds(pl.multiple_of((1 - core) * SLICE, 64), pad), :] = jnp.zeros((2, pad, 1024), BF)
    top = pl.ds(pl.multiple_of(core * pad, 64), SLICE)
    for h in range(8):
        for g in range(2):
            col = pl.multiple_of(lax.rem(h // 2 + 4 - zh, 4) * 256 + g * SLAB, SLAB)
            w_new[h % 2, top, pl.ds(col, SLAB)] = w_wide[pl.ds(2 * h + g, SLICE, stride=16), :].astype(BF)

    def sx_copy(n):
        return remote(sx_send.at[n], sx_recv.at[n], sxs.at[n], sxr.at[n], sibling)

    def rf_copy(n, i):
        return remote(rf_send.at[n, i], rf_recv.at[n, i], rfs.at[n, i], rfr.at[n, i], zh_dev(1 + 2 * i))

    def rn_copy(n, i):
        return remote(rn_send.at[n, i], rn_recv.at[n, i], rns.at[n, i], rnr.at[n, i], zh_dev(1 + 2 * i))

    def act_part(n):
        for r in range(4 * n, min(4 * n + 4, 15)):
            message(1, send_new, recv_new, r).wait_recv()
        rows = [take(recv_new, n, h, WIN // 2) for h in range(2)]

        def part(c):
            return sum(dot(rows[h], w_new[c, h * (WIN // 2) : (h + 1) * (WIN // 2), :]) for h in range(2))

        sx_send[n] = part(1 - core).astype(BF)
        sx_copy(n).start()
        pn[n] = part(core)

    def act_far(n):
        sx_copy(n).wait_recv()
        total = pn[n] + sx_recv[n].astype(F32)
        for i in range(2):
            rf_send[n, i] = total[i * CH // 2 : (i + 1) * CH // 2, 512:768].astype(BF)
            rf_copy(n, i).start()
        pn[n] = total

    def act_near(n):
        for i in range(2):
            rf_copy(n, i).wait_recv()
            cols = slice(256 + 512 * i, 512 + 512 * i)
            own, more = slice((1 - i) * CH // 2, (2 - i) * CH // 2), slice(i * CH // 2, (i + 1) * CH // 2)
            rn_send[n, i, own, :] = pn[n, own, cols].astype(BF)
            rn_send[n, i, more, :] = (pn[n, more, cols] + rf_recv[n, i].astype(F32)).astype(BF)
            rn_copy(n, i).start()

    def so_copy(b, n):
        return remote(so_send.at[b, n], so_recv.at[b, n], sos.at[b, n], sor.at[b, n], sibling)

    def down(b, n, act):
        gate = act[:, :SLAB]
        hidden = (gate / (1.0 + jnp.exp(-gate)) * act[:, SLAB:]).astype(BF)
        so_send[b, n] = dot(hidden, w_out[:, pl.ds(other, HALF)]).astype(BF)
        so_copy(b, n).start()
        po[b, n] = dot(hidden, w_out[:, pl.ds(half, HALF)])

    def back(b, part, r):
        src, land = ((ra_send, ra_recv), (rb_send, rb_recv))[part]
        return remote(src.at[b, r], land.at[b, r], rts.at[b, part, r], rtr.at[b, part, r], from_dev(r))

    def chip_sum(b, n):
        so_copy(b, n).wait_recv()
        total = po[b, n] + so_recv[b, n].astype(F32)
        put(ra_send.at[b], n, total[:, : 2 * PART_A], PART_A)
        put(rb_send.at[b], n, total[:, 2 * PART_A :], PART_B)

    def send_back(b, part, n):
        for r in range(4 * n, 4 * n + 4):
            if r < 15:
                back(b, part, r).start()
            elif part == 0:
                ra_recv[b, 15] = ra_send[b, 15]
            else:
                rb_recv[b, 15] = rb_send[b, 15]

    for n in range(5):
        if n < 4:
            act_part(n)
        if n >= 1:
            act_far(n - 1)

    for n in range(2, 4):
        for r in range(4 * n - 8, 4 * n - 4):
            message(0, send_old, recv_old, r).wait_send()
        send_out(0, send_old, recv_old, n)

    def fwd_copy(r):
        return remote(recv_old.at[r], sib_old.at[r], fs.at[r], fr.at[r], sibling)

    def forward(n):
        for r in range(4 * n, 4 * n + 4):
            if r < 15:
                message(0, send_old, recv_old, r).wait_recv()
            fwd_copy(r).start()

    def act_old(n):
        act = jnp.zeros((CH, 2 * SLAB), F32)
        for h in range(2):
            at = pl.ds(pl.multiple_of(half + h * BLK, 128), BLK)
            act += dot(take(recv_old, n, h, BLK), w_old[at, :])
        for r in range(4 * n, 4 * n + 4):
            fwd_copy(r).wait_recv()
        for h in range(2):
            at = pl.ds(pl.multiple_of(other + h * BLK, 128), BLK)
            act += dot(take(sib_old, n, h, BLK), w_old[at, :])
        down(0, n, act)

    loads[1].wait()
    w_wide[...] = w_raw[1].astype(F32)
    for g in range(2):
        w_old[:, g * SLAB : (g + 1) * SLAB] = w_wide[pl.ds(g, D, stride=2), :].astype(BF)
    loads[2].wait()

    for n in range(6):
        if n < 4:
            forward(n)
            act_near(n)
        if 1 <= n < 5:
            act_old(n - 1)
        if n >= 2:
            chip_sum(0, n - 2)
            send_back(0, 0, n - 2)
            send_back(0, 1, n - 2)

    def act_new(n):
        act = pn[n, :, 0:256]
        for i in range(2):
            rn_copy(n, i).wait_recv()
            act += rn_recv[n, i].astype(F32)
        down(1, n, act)

    for n in range(5):
        if n < 4:
            act_new(n)
        if 1 <= n < 5:
            chip_sum(1, n - 1)
            send_back(1, 0, n - 1)

    for n in range(4):
        send_back(1, 1, n)

    def z1_copy(b, part, o):
        at = pl.ds(pl.multiple_of(lax.rem(zl + zoff[o], 4) * ROWS, ROWS), ROWS)
        col, width = PARTS[part]
        cols = slice(col, col + 2 * width)
        return remote(
            z1_send.at[b, at, cols], z1_recv.at[b, o, :, cols],
            z1s.at[b, part, o], z1r.at[b, part, o], z_dev(zoff[o]),
        )

    def combine(b, part):
        for r in range(15):
            back(b, part, r).wait_recv()
        col, width = PARTS[part]
        for h in range(2):
            rows = (ra_recv, rb_recv)[part][b, :, h * SLOTS : (h + 1) * SLOTS, :]
            rows = rows.astype(F32).reshape(16 * SLOTS, width).astype(BF)
            total = dot(comb[b, 0], rows) + dot(comb[b, 1], rows)
            cols = slice(col + h * width, col + (h + 1) * width)
            z1_own[b, :, cols] = total
            z1_send[b, :, cols] = total.astype(BF)
        for o in range(3):
            z1_copy(b, part, o).start()

    def z2_copy(b, t):
        k, c = t // 2, t % 2
        return remote(
            z2_send.at[b, :, k * 896 + c * 384 : k * 896 + c * 384 + WIN], z2_recv.at[b, zh],
            z2s.at[b, t], z2r.at[b, zh], {"rep": (2 * core + k) * 2 + c, "ep": ep},
        )

    def is_self(t):
        return rep == (2 * core + t // 2) * 2 + t % 2

    def spread(b, part):
        col, width = PARTS[part]
        cols = slice(col, col + 2 * width)
        total = z1_own[b, mine, cols]
        for o in range(3):
            z1_copy(b, part, o).wait_recv()
            total += z1_recv[b, o, :, cols].astype(F32)
        z2_send[b, :, cols] = total.astype(BF)
        for t in (2 * part, 2 * part + 1):
            k, c = t // 2, t % 2

            @pl.when(jnp.logical_not(is_self(t)))
            def _():
                z2_copy(b, t).start()

            @pl.when(is_self(t))
            def _():
                z2_recv[b, zh] = z2_send[b, :, k * 896 + c * 384 : k * 896 + c * 384 + WIN]

    def finish(b, out):
        for s in range(4):

            @pl.when(jnp.logical_not((zh == s) & (core == zh // 2)))
            def _():
                ref = z2_recv.at[b, s]
                remote(ref, ref, z2s.at[b, 0], z2r.at[b, s], sibling).wait_recv()

        total = sum(z2_recv[b, s].astype(F32) for s in range(4))
        result[b] = jnp.where(core == 0, total[:, :SLICE], total[:, WIN - SLICE :]).astype(BF)
        pltpu.make_async_copy(result.at[b], out, ins.at[b]).start()

    combine(0, 0)
    combine(0, 1)
    spread(0, 0)
    spread(0, 1)
    combine(1, 0)
    spread(1, 0)
    combine(1, 1)
    finish(0, out_old)
    spread(1, 1)
    finish(1, out_new)

    for b, out in enumerate((out_old, out_new)):
        pltpu.make_async_copy(result.at[b], out, ins.at[b]).wait()

    for o in range(3):
        for kind in range(3):
            z_copy(o, kind).wait_send()
        for b in range(2):
            for part in range(2):
                z1_copy(b, part, o).wait_send()
    for n in range(4):
        sx_copy(n).wait_send()
        for i in range(2):
            rf_copy(n, i).wait_send()
            rn_copy(n, i).wait_send()
        for b in range(2):
            so_copy(b, n).wait_send()
    for r in range(16):
        fwd_copy(r).wait_send()
    for r in range(15):
        if r >= 8:
            message(0, send_old, recv_old, r).wait_send()
        message(1, send_new, recv_new, r).wait_send()
        for b in range(2):
            for part in range(2):
                back(b, part, r).wait_send()
    for b in range(2):
        for t in range(4):

            @pl.when(jnp.logical_not(is_self(t)))
            def _():
                z2_copy(b, t).wait_send()


def body(rows_old, rows_new, routes_old, routes_new, gates_old, gates_new, w_in_old, w_in_new, w_out):
    w_old = w_in_old[0].reshape(2 * D, SLAB)
    w_new = w_in_new[0].reshape(SLICE, 2, 8, SLAB).transpose(0, 2, 1, 3).reshape(SLICE * 16, SLAB)
    hbm = pl.BlockSpec(memory_space=pl.ANY)
    dma = pltpu.SemaphoreType.DMA
    out = jax.ShapeDtypeStruct((ROWS, SLICE), BF)
    return pl.pallas_call(
        kernel,
        out_shape=(out, out),
        in_specs=[hbm] * 9,
        out_specs=(hbm, hbm),
        scratch_shapes=[
            pltpu.VMEM((2, TOPK, ROWS), jnp.int32),
            pltpu.VMEM((2, TOPK, ROWS), F32),
            pltpu.VMEM((2, ROWS, SLICE), BF),
            pltpu.VMEM((2, 2 * D, SLAB), BF),
            pltpu.VMEM((2 * D, SLAB), F32),
            pltpu.VMEM((D, 2 * SLAB), BF),
            pltpu.VMEM((2, WIN, 1024), BF),
            pltpu.VMEM((SLAB, D), BF),
            pltpu.VMEM((128, 128), F32),
            pltpu.VMEM((4 * ROWS, 128), F32),
            pltpu.VMEM((4 * ROWS, HALF), BF),
            pltpu.VMEM((4 * ROWS, WIN), BF),
            pltpu.VMEM((2, 16 * SLOTS, 128), BF),
            pltpu.VMEM((2, 2, 128, 16 * SLOTS), BF),
            pltpu.VMEM((16, 2 * SLOTS, WIN // 2), BF),
            pltpu.VMEM((16, 2 * SLOTS, WIN // 2), BF),
            pltpu.VMEM((16, 2 * SLOTS, BLK), BF),
            pltpu.VMEM((16, 2 * SLOTS, BLK), BF),
            pltpu.VMEM((16, 2 * SLOTS, BLK), BF),
            pltpu.VMEM((4, CH, 1024), F32),
            pltpu.VMEM((4, CH, 1024), BF),
            pltpu.VMEM((4, CH, 1024), BF),
            pltpu.VMEM((4, 2, CH // 2, 256), BF),
            pltpu.VMEM((4, 2, CH // 2, 256), BF),
            pltpu.VMEM((4, 2, CH, 256), BF),
            pltpu.VMEM((4, 2, CH, 256), BF),
            pltpu.VMEM((2, 4, CH, HALF), F32),
            pltpu.VMEM((2, 4, CH, HALF), BF),
            pltpu.VMEM((2, 4, CH, HALF), BF),
            pltpu.VMEM((2, 16, 2 * SLOTS, PART_A), BF),
            pltpu.VMEM((2, 16, 2 * SLOTS, PART_A), BF),
            pltpu.VMEM((2, 16, 2 * SLOTS, PART_B), BF),
            pltpu.VMEM((2, 16, 2 * SLOTS, PART_B), BF),
            pltpu.VMEM((2, 4 * ROWS, HALF), F32),
            pltpu.VMEM((2, 4 * ROWS, HALF), BF),
            pltpu.VMEM((2, 3, ROWS, HALF), BF),
            pltpu.VMEM((2, ROWS, HALF), BF),
            pltpu.VMEM((2, 4, ROWS, WIN), BF),
            dma((6,)),
            dma((3,)),
            dma((3, 3)), dma((3, 3)),
            dma((2, 16)), dma((2, 16)),
            dma((16,)), dma((16,)),
            dma((4,)), dma((4,)),
            dma((4, 2)), dma((4, 2)),
            dma((4, 2)), dma((4, 2)),
            dma((2, 4)), dma((2, 4)),
            dma((2, 2, 16)), dma((2, 2, 16)),
            dma((2, 2, 3)), dma((2, 2, 3)),
            dma((2, 4)), dma((2, 4)),
        ],
        compiler_params=pltpu.CompilerParams(
            collective_id=0, has_side_effects=True, vmem_limit_bytes=60 * 1024 * 1024
        ),
    )(routes_old.T, routes_new.T, gates_old.T, gates_new.T, rows_old, rows_new, w_old, w_new, w_out[0])


def solution(mesh):
    return jax.shard_map(
        body,
        mesh=mesh,
        in_specs=(
            P("ep", None),
            P("ep", None),
            P("ep", None),
            P("ep", None),
            P("ep", None),
            P("ep", None),
            P("ep", None, None, "rep"),
            P("ep", "rep", None, None),
            P("ep", "rep", None),
        ),
        out_specs=(P("ep", "rep"), P("ep", "rep")),
        check_vma=False,
    )
```

```python
import functools

import jax
import jax.numpy as jnp
from jax import lax
from jax.experimental import pallas as pl
from jax.experimental.pallas import tpu as pltpu
from jax.sharding import PartitionSpec as P

BF = jnp.bfloat16
F32 = jnp.float32
MESH = pl.DeviceIdType.MESH

D = 3584
HALF = D // 2
BLK = HALF // 2
WIN = 512
SLICE = 448
SLAB = 128
TOPK = 8
ROWS = 32
CAP = 6
SLOTS = 4 * CAP
CH = 4 * SLOTS
FAR = (2, 1, 3, 0)
PLACE = tuple((dx, (total - dx) % 4) for total in FAR for dx in FAR)
PART_A, PART_B = 512, 384
PARTS = ((0, PART_A), (2 * PART_A, PART_B))


def dot(a, b):
    return lax.dot_general(a, b, (((1,), (0,)), ((), ())), preferred_element_type=F32)


def dot_nt(a, b):
    return lax.dot_general(a, b, (((1,), (1,)), ((), ())), preferred_element_type=F32)


def iota(shape, dim):
    return lax.broadcasted_iota(jnp.int32, shape, dim)


def by24(q):
    return (q * 2731) >> 16


def by6(q):
    return (q * 10923) >> 16


def far(m):
    return jnp.where(m == 0, 2, jnp.where(m == 3, 0, 2 * m - 1))


def kernel(
    ro_t, rn_t, go_t, gn_t, rows_old, rows_new, w_old_hbm, w_new_hbm, w_out_hbm,
    out_old, out_new,
    tab_i, tab_f, result,
    w_raw, w_wide, w_old, w_new, w_out, square, meta_z, rz_old, rz_new, disp, comb,
    send_new, recv_new, send_old, recv_old, sib_old,
    pn, sx_send, sx_recv, rf_send, rf_recv, rn_send, rn_recv,
    po, so_send, so_recv, ra_send, ra_recv, rb_send, rb_recv,
    z1_own, z1_send, z1_recv, z2_send, z2_recv,
    ins, ws, zs, zr, xs, xr, fs, fr, sxs, sxr, rfs, rfr, rns, rnr, sos, sor, rts, rtr, z1s, z1r, z2s, z2r,
):
    ep = lax.axis_index("ep")
    rep = lax.axis_index("rep")
    core, zh = lax.rem(rep, 2), rep // 2
    zl, me = lax.rem(ep, 4), ep // 4
    x, y = me // 4, lax.rem(me, 4)
    z = zh * 4 + zl
    zoff = (1, 15, 2 + 12 * core)

    def z_dev(offset):
        t = lax.rem(z + offset, 16)
        return {"rep": (t // 4) * 2 + core, "ep": me * 4 + lax.rem(t, 4)}

    def to_dev(r):
        dx, dy = PLACE[r]
        return {"rep": rep, "ep": (lax.rem(x + dx, 4) * 4 + lax.rem(y + dy, 4)) * 4 + zl}

    def from_dev(r):
        dx, dy = PLACE[r]
        return {"rep": rep, "ep": (lax.rem(x + 4 - dx, 4) * 4 + lax.rem(y + 4 - dy, 4)) * 4 + zl}

    def zh_dev(k):
        return {"rep": lax.rem(zh + k, 4) * 2 + core, "ep": ep}

    sibling = {"rep": zh * 2 + (1 - core), "ep": ep}

    def remote(src, dst, ss, rs, dev):
        return pltpu.make_async_remote_copy(
            src_ref=src, dst_ref=dst, send_sem=ss, recv_sem=rs, device_id=dev, device_id_type=MESH
        )

    half = pl.multiple_of(core * HALF, 128)
    other = pl.multiple_of((1 - core) * HALF, 128)
    mine = pl.ds(pl.multiple_of(zl * ROWS, ROWS), ROWS)
    window = pl.ds(pl.multiple_of(zh * 896 + core * 384, 128), WIN)
    inputs = [
        pltpu.make_async_copy(src, dst, ins.at[i])
        for i, (src, dst) in enumerate(
            (
                (ro_t, tab_i.at[0]), (rn_t, tab_i.at[1]), (go_t, tab_f.at[0]), (gn_t, tab_f.at[1]),
                (rows_new.at[:, window], rz_new.at[mine, :]),
                (rows_old.at[:, pl.ds(half, HALF)], rz_old.at[mine, :]),
            )
        )
    ]
    for copy in inputs:
        copy.start()

    barrier = pltpu.get_barrier_semaphore()
    for r in range(15):
        pl.semaphore_signal(barrier, 1, device_id=to_dev(r), device_id_type=MESH)
    for o in (1, 15, 2, 14):
        pl.semaphore_signal(barrier, 1, device_id=z_dev(o), device_id_type=MESH)
    for k in range(1, 8):
        pl.semaphore_signal(
            barrier, 1, device_id={"rep": lax.rem(rep + k, 8), "ep": ep}, device_id_type=MESH
        )
    loads = [
        pltpu.make_async_copy(src, dst, ws.at[i])
        for i, (src, dst) in enumerate(
            ((w_new_hbm, w_raw.at[0]), (w_old_hbm, w_raw.at[1]), (w_out_hbm, w_out))
        )
    ]
    for load in loads:
        load.start()

    square[...] = jnp.zeros((128, 128), F32)
    for copy in inputs[:4]:
        copy.wait()
    for i, table in enumerate((tab_i.at[0], tab_i.at[1], tab_f.at[0], tab_f.at[1])):
        square[8 * i : 8 * i + 8, 0:ROWS] = table[...].astype(F32)
    meta_z[mine, :] = square[...].T[:ROWS, :]

    lane = iota((4 * ROWS, 128), 1)
    p_row, p_col = iota((4 * ROWS, 4 * ROWS), 0), iota((4 * ROWS, 4 * ROWS), 1)
    before = jnp.where((p_col < p_row) & (p_col >> 5 == p_row >> 5), 1.0, 0.0).astype(BF)
    qs = iota((16 * SLOTS, 128), 0)
    rq = by24(qs)
    dx = far(rq & 3)
    dy = (far(rq >> 2) - dx) & 3
    expert = (((x + dx) & 3) * 4 + ((y + dy) & 3)) * 4 + zl
    pick = jnp.where(expert == iota((16 * SLOTS, 128), 1), 1.0, 0.0).astype(BF)
    in_q = qs - by24(qs) * 24
    slot_q = (in_q - by6(in_q) * 6).astype(F32)
    same_q = by6(in_q) == iota((16 * SLOTS, 128), 1) >> 5
    ql = iota((128, 16 * SLOTS), 1)
    in_l = ql - by24(ql) * 24
    slot_l = (in_l - by6(in_l) * 6).astype(F32)
    same_l = by6(in_l) == iota((128, 16 * SLOTS), 0) >> 5
    pl.semaphore_wait(barrier, 26)

    def z_copy(o, kind):
        offset = zoff[o]
        there = lax.rem(z + offset, 16) // 4
        if kind == 0:
            src, land = meta_z.at[mine, :], meta_z
        elif kind == 1:
            theirs = pl.ds(pl.multiple_of(there * 896 + core * 384, 128), WIN)
            src, land = rows_new.at[:, theirs], rz_new
        else:
            src, land = rows_old.at[:, pl.ds(half, HALF)], rz_old
        return remote(src, land.at[mine, :], zs.at[kind, o], zr.at[kind, o], z_dev(offset))

    def z_from(o, kind, buf):
        src = lax.rem(zl + 16 - zoff[o], 4)
        ref = buf.at[pl.ds(pl.multiple_of(src * ROWS, ROWS), ROWS), :]
        return remote(ref, ref, zs.at[kind, o], zr.at[kind, o], z_dev(zoff[o]))

    for kind in range(3):
        for o in range(3):
            z_copy(o, kind).start()
    for o in range(3):
        z_from(o, 0, meta_z).wait_recv()

    def tables(b):
        named = jnp.zeros((4 * ROWS, 128), F32)
        gate = jnp.zeros((4 * ROWS, 128), F32)
        for k in range(TOPK):
            hit = meta_z[:, 8 * b + k : 8 * b + k + 1].astype(jnp.int32) == lane
            named = named + jnp.where(hit, 1.0, 0.0)
            gate = gate + jnp.where(hit, meta_z[:, 16 + 8 * b + k : 17 + 8 * b + k], 0.0)
        rank = dot(before, named.astype(BF))
        code = jnp.where(named > 0.5, rank, -1.0).astype(BF)
        disp[b] = jnp.where((dot_nt(pick, code) == slot_q) & same_q, 1.0, 0.0).astype(BF)
        chosen = (dot_nt(code, pick) == slot_l) & same_l
        high = gate.astype(BF)
        low = (gate - high.astype(F32)).astype(BF)
        comb[b, 0] = jnp.where(chosen, dot_nt(high, pick), 0.0).astype(BF)
        comb[b, 1] = jnp.where(chosen, dot_nt(low, pick), 0.0).astype(BF)

    def message(b, buf, land, r):
        return remote(buf.at[r], land.at[r], xs.at[b, r // 4], xr.at[b, r // 4], to_dev(r))

    def others(n):
        return slice(4 * n, min(4 * n + 4, 15))

    def chunk(b, buf, land, n):
        at = others(n)
        return remote(buf.at[at], land.at[at], xs.at[b, n], xr.at[b, n], sibling)

    def put(buf, n, value, width):
        v = value.reshape(4, SLOTS, 2 * width)
        buf[4 * n : 4 * n + 4, 0:SLOTS, :] = v[:, :, :width].astype(BF)
        buf[4 * n : 4 * n + 4, SLOTS : 2 * SLOTS, :] = v[:, :, width:].astype(BF)

    def take(buf, n, h, width):
        v = buf[4 * n : 4 * n + 4, h * SLOTS : (h + 1) * SLOTS, :]
        return v.astype(F32).reshape(CH, width).astype(BF)

    def send_out(b, buf, land, n):
        for r in range(4 * n, 4 * n + 4):
            if r < 15:
                message(b, buf, land, r).start()
            else:
                land[15] = buf[15]

    def dispatch(b, rz, buf, land, width, ahead):
        for n in range(4):
            put(buf, n, dot(disp[b, n * CH : (n + 1) * CH, :], rz[...]), width)
            if n < ahead:
                send_out(b, buf, land, n)

    tables(1)
    for o in range(3):
        z_from(o, 1, rz_new).wait_recv()
    inputs[4].wait()
    dispatch(1, rz_new, send_new, recv_new, WIN // 2, 4)
    tables(0)
    for o in range(3):
        z_from(o, 2, rz_old).wait_recv()
    inputs[5].wait()
    dispatch(0, rz_old, send_old, recv_old, BLK, 2)

    loads[0].wait()
    w_wide[...] = w_raw[0].astype(F32)
    pad = WIN - SLICE
    w_new[:, pl.ds(pl.multiple_of((1 - core) * SLICE, 64), pad), :] = jnp.zeros((2, pad, 1024), BF)
    top = pl.ds(pl.multiple_of(core * pad, 64), SLICE)
    for h in range(8):
        for g in range(2):
            col = pl.multiple_of(lax.rem(h // 2 + 4 - zh, 4) * 256 + g * SLAB, SLAB)
            w_new[h % 2, top, pl.ds(col, SLAB)] = w_wide[pl.ds(2 * h + g, SLICE, stride=16), :].astype(BF)

    def sx_copy(n):
        return remote(sx_send.at[n], sx_recv.at[n], sxs.at[n], sxr.at[n], sibling)

    def rf_copy(n, i):
        return remote(rf_send.at[n, i], rf_recv.at[n, i], rfs.at[n, i], rfr.at[n, i], zh_dev(1 + 2 * i))

    def rn_copy(n, i):
        return remote(rn_send.at[n, i], rn_recv.at[n, i], rns.at[n, i], rnr.at[n, i], zh_dev(1 + 2 * i))

    def act_part(n):
        chunk(1, send_new, recv_new, n).wait_recv()
        rows = [take(recv_new, n, h, WIN // 2) for h in range(2)]

        def part(c):
            return sum(dot(rows[h], w_new[c, h * (WIN // 2) : (h + 1) * (WIN // 2), :]) for h in range(2))

        sx_send[n] = part(1 - core).astype(BF)
        sx_copy(n).start()
        pn[n] = part(core)

    def act_far(n):
        sx_copy(n).wait_recv()
        total = pn[n] + sx_recv[n].astype(F32)
        for i in range(2):
            rf_send[n, i] = total[i * CH // 2 : (i + 1) * CH // 2, 512:768].astype(BF)
            rf_copy(n, i).start()
        pn[n] = total

    def act_near(n):
        for i in range(2):
            rf_copy(n, i).wait_recv()
            cols = slice(256 + 512 * i, 512 + 512 * i)
            own, more = slice((1 - i) * CH // 2, (2 - i) * CH // 2), slice(i * CH // 2, (i + 1) * CH // 2)
            rn_send[n, i, own, :] = pn[n, own, cols].astype(BF)
            rn_send[n, i, more, :] = (pn[n, more, cols] + rf_recv[n, i].astype(F32)).astype(BF)
            rn_copy(n, i).start()

    def so_copy(b, n):
        return remote(so_send.at[b, n], so_recv.at[b, n], sos.at[b, n], sor.at[b, n], sibling)

    def down(b, n, act):
        gate = act[:, :SLAB]
        hidden = (gate / (1.0 + jnp.exp(-gate)) * act[:, SLAB:]).astype(BF)
        so_send[b, n] = dot(hidden, w_out[:, pl.ds(other, HALF)]).astype(BF)
        so_copy(b, n).start()
        po[b, n] = dot(hidden, w_out[:, pl.ds(half, HALF)])

    def back(b, part, r):
        src, land = ((ra_send, ra_recv), (rb_send, rb_recv))[part]
        n = r // 4
        return remote(src.at[b, r], land.at[b, r], rts.at[b, part, n], rtr.at[b, part, n], from_dev(r))

    def back_chunk(b, part, n):
        src, land = ((ra_send, ra_recv), (rb_send, rb_recv))[part]
        at = others(n)
        return remote(src.at[b, at], land.at[b, at], rts.at[b, part, n], rtr.at[b, part, n], sibling)

    def chip_sum(b, n):
        so_copy(b, n).wait_recv()
        total = po[b, n] + so_recv[b, n].astype(F32)
        put(ra_send.at[b], n, total[:, : 2 * PART_A], PART_A)
        put(rb_send.at[b], n, total[:, 2 * PART_A :], PART_B)

    def send_back(b, part, n):
        for r in range(4 * n, 4 * n + 4):
            if r < 15:
                back(b, part, r).start()
            elif part == 0:
                ra_recv[b, 15] = ra_send[b, 15]
            else:
                rb_recv[b, 15] = rb_send[b, 15]

    for n in range(5):
        if n < 4:
            act_part(n)
        if n >= 1:
            act_far(n - 1)

    for n in range(2, 4):
        chunk(0, send_old, recv_old, n - 2).wait_send()
        send_out(0, send_old, recv_old, n)

    def fwd_copy(n):
        at = slice(4 * n, 4 * n + 4)
        return remote(recv_old.at[at], sib_old.at[at], fs.at[n], fr.at[n], sibling)

    def forward(n):
        chunk(0, send_old, recv_old, n).wait_recv()
        fwd_copy(n).start()

    def act_old(n):
        act = jnp.zeros((CH, 2 * SLAB), F32)
        for h in range(2):
            at = pl.ds(pl.multiple_of(half + h * BLK, 128), BLK)
            act += dot(take(recv_old, n, h, BLK), w_old[at, :])
        fwd_copy(n).wait_recv()
        for h in range(2):
            at = pl.ds(pl.multiple_of(other + h * BLK, 128), BLK)
            act += dot(take(sib_old, n, h, BLK), w_old[at, :])
        down(0, n, act)

    loads[1].wait()
    w_wide[...] = w_raw[1].astype(F32)
    for g in range(2):
        w_old[:, g * SLAB : (g + 1) * SLAB] = w_wide[pl.ds(g, D, stride=2), :].astype(BF)
    loads[2].wait()

    for n in range(6):
        if n < 4:
            forward(n)
            act_near(n)
        if 1 <= n < 5:
            act_old(n - 1)
        if n >= 2:
            chip_sum(0, n - 2)
            send_back(0, 0, n - 2)
            send_back(0, 1, n - 2)

    def act_new(n):
        act = pn[n, :, 0:256]
        for i in range(2):
            rn_copy(n, i).wait_recv()
            act += rn_recv[n, i].astype(F32)
        down(1, n, act)

    for n in range(5):
        if n < 4:
            act_new(n)
        if 1 <= n < 5:
            chip_sum(1, n - 1)
            send_back(1, 0, n - 1)

    for n in range(4):
        send_back(1, 1, n)

    def z1_copy(b, part, o):
        at = pl.ds(pl.multiple_of(lax.rem(zl + zoff[o], 4) * ROWS, ROWS), ROWS)
        col, width = PARTS[part]
        cols = slice(col, col + 2 * width)
        return remote(
            z1_send.at[b, at, cols], z1_recv.at[b, o, :, cols],
            z1s.at[b, part, o], z1r.at[b, part, o], z_dev(zoff[o]),
        )

    def combine(b, part):
        for n in range(4):
            back_chunk(b, part, n).wait_recv()
        col, width = PARTS[part]
        for h in range(2):
            rows = (ra_recv, rb_recv)[part][b, :, h * SLOTS : (h + 1) * SLOTS, :]
            rows = rows.astype(F32).reshape(16 * SLOTS, width).astype(BF)
            total = dot(comb[b, 0], rows) + dot(comb[b, 1], rows)
            cols = slice(col + h * width, col + (h + 1) * width)
            z1_own[b, :, cols] = total
            z1_send[b, :, cols] = total.astype(BF)
        for o in range(3):
            z1_copy(b, part, o).start()

    def z2_copy(b, t):
        k, c = t // 2, t % 2
        return remote(
            z2_send.at[b, :, k * 896 + c * 384 : k * 896 + c * 384 + WIN], z2_recv.at[b, zh],
            z2s.at[b, t], z2r.at[b, zh], {"rep": (2 * core + k) * 2 + c, "ep": ep},
        )

    def is_self(t):
        return rep == (2 * core + t // 2) * 2 + t % 2

    def spread(b, part):
        col, width = PARTS[part]
        cols = slice(col, col + 2 * width)
        total = z1_own[b, mine, cols]
        for o in range(3):
            z1_copy(b, part, o).wait_recv()
            total += z1_recv[b, o, :, cols].astype(F32)
        z2_send[b, :, cols] = total.astype(BF)
        for t in (2 * part, 2 * part + 1):
            k, c = t // 2, t % 2

            @pl.when(jnp.logical_not(is_self(t)))
            def _():
                z2_copy(b, t).start()

            @pl.when(is_self(t))
            def _():
                z2_recv[b, zh] = z2_send[b, :, k * 896 + c * 384 : k * 896 + c * 384 + WIN]

    def finish(b, out):
        for s in range(4):

            @pl.when(jnp.logical_not((zh == s) & (core == zh // 2)))
            def _():
                ref = z2_recv.at[b, s]
                remote(ref, ref, z2s.at[b, 0], z2r.at[b, s], sibling).wait_recv()

        total = sum(z2_recv[b, s].astype(F32) for s in range(4))
        result[b] = jnp.where(core == 0, total[:, :SLICE], total[:, WIN - SLICE :]).astype(BF)
        pltpu.make_async_copy(result.at[b], out, ins.at[b]).start()

    combine(0, 0)
    combine(0, 1)
    spread(0, 0)
    spread(0, 1)
    combine(1, 0)
    spread(1, 0)
    combine(1, 1)
    finish(0, out_old)
    spread(1, 1)
    finish(1, out_new)

    for b, out in enumerate((out_old, out_new)):
        pltpu.make_async_copy(result.at[b], out, ins.at[b]).wait()

    for o in range(3):
        for kind in range(3):
            z_copy(o, kind).wait_send()
        for b in range(2):
            for part in range(2):
                z1_copy(b, part, o).wait_send()
    for n in range(4):
        sx_copy(n).wait_send()
        for i in range(2):
            rf_copy(n, i).wait_send()
            rn_copy(n, i).wait_send()
        for b in range(2):
            so_copy(b, n).wait_send()
    for n in range(4):
        fwd_copy(n).wait_send()
        if n >= 2:
            chunk(0, send_old, recv_old, n).wait_send()
        chunk(1, send_new, recv_new, n).wait_send()
        for b in range(2):
            for part in range(2):
                back_chunk(b, part, n).wait_send()
    for b in range(2):
        for t in range(4):

            @pl.when(jnp.logical_not(is_self(t)))
            def _():
                z2_copy(b, t).wait_send()


def body(rows_old, rows_new, routes_old, routes_new, gates_old, gates_new, w_in_old, w_in_new, w_out):
    w_old = w_in_old[0].reshape(2 * D, SLAB)
    w_new = w_in_new[0].reshape(SLICE, 2, 8, SLAB).transpose(0, 2, 1, 3).reshape(SLICE * 16, SLAB)
    hbm = pl.BlockSpec(memory_space=pl.ANY)
    dma = pltpu.SemaphoreType.DMA
    out = jax.ShapeDtypeStruct((ROWS, SLICE), BF)
    return pl.pallas_call(
        kernel,
        out_shape=(out, out),
        in_specs=[hbm] * 9,
        out_specs=(hbm, hbm),
        scratch_shapes=[
            pltpu.VMEM((2, TOPK, ROWS), jnp.int32),
            pltpu.VMEM((2, TOPK, ROWS), F32),
            pltpu.VMEM((2, ROWS, SLICE), BF),
            pltpu.VMEM((2, 2 * D, SLAB), BF),
            pltpu.VMEM((2 * D, SLAB), F32),
            pltpu.VMEM((D, 2 * SLAB), BF),
            pltpu.VMEM((2, WIN, 1024), BF),
            pltpu.VMEM((SLAB, D), BF),
            pltpu.VMEM((128, 128), F32),
            pltpu.VMEM((4 * ROWS, 128), F32),
            pltpu.VMEM((4 * ROWS, HALF), BF),
            pltpu.VMEM((4 * ROWS, WIN), BF),
            pltpu.VMEM((2, 16 * SLOTS, 128), BF),
            pltpu.VMEM((2, 2, 128, 16 * SLOTS), BF),
            pltpu.VMEM((16, 2 * SLOTS, WIN // 2), BF),
            pltpu.VMEM((16, 2 * SLOTS, WIN // 2), BF),
            pltpu.VMEM((16, 2 * SLOTS, BLK), BF),
            pltpu.VMEM((16, 2 * SLOTS, BLK), BF),
            pltpu.VMEM((16, 2 * SLOTS, BLK), BF),
            pltpu.VMEM((4, CH, 1024), F32),
            pltpu.VMEM((4, CH, 1024), BF),
            pltpu.VMEM((4, CH, 1024), BF),
            pltpu.VMEM((4, 2, CH // 2, 256), BF),
            pltpu.VMEM((4, 2, CH // 2, 256), BF),
            pltpu.VMEM((4, 2, CH, 256), BF),
            pltpu.VMEM((4, 2, CH, 256), BF),
            pltpu.VMEM((2, 4, CH, HALF), F32),
            pltpu.VMEM((2, 4, CH, HALF), BF),
            pltpu.VMEM((2, 4, CH, HALF), BF),
            pltpu.VMEM((2, 16, 2 * SLOTS, PART_A), BF),
            pltpu.VMEM((2, 16, 2 * SLOTS, PART_A), BF),
            pltpu.VMEM((2, 16, 2 * SLOTS, PART_B), BF),
            pltpu.VMEM((2, 16, 2 * SLOTS, PART_B), BF),
            pltpu.VMEM((2, 4 * ROWS, HALF), F32),
            pltpu.VMEM((2, 4 * ROWS, HALF), BF),
            pltpu.VMEM((2, 3, ROWS, HALF), BF),
            pltpu.VMEM((2, ROWS, HALF), BF),
            pltpu.VMEM((2, 4, ROWS, WIN), BF),
            dma((6,)),
            dma((3,)),
            dma((3, 3)), dma((3, 3)),
            dma((2, 4)), dma((2, 4)),
            dma((4,)), dma((4,)),
            dma((4,)), dma((4,)),
            dma((4, 2)), dma((4, 2)),
            dma((4, 2)), dma((4, 2)),
            dma((2, 4)), dma((2, 4)),
            dma((2, 2, 4)), dma((2, 2, 4)),
            dma((2, 2, 3)), dma((2, 2, 3)),
            dma((2, 4)), dma((2, 4)),
        ],
        compiler_params=pltpu.CompilerParams(
            collective_id=0, has_side_effects=True, vmem_limit_bytes=60 * 1024 * 1024
        ),
    )(routes_old.T, routes_new.T, gates_old.T, gates_new.T, rows_old, rows_new, w_old, w_new, w_out[0])


def solution(mesh):
    return jax.shard_map(
        body,
        mesh=mesh,
        in_specs=(
            P("ep", None),
            P("ep", None),
            P("ep", None),
            P("ep", None),
            P("ep", None),
            P("ep", None),
            P("ep", None, None, "rep"),
            P("ep", "rep", None, None),
            P("ep", "rep", None),
        ),
        out_specs=(P("ep", "rep"), P("ep", "rep")),
        check_vma=False,
    )
```

```python
import functools

import jax
import jax.numpy as jnp
from jax import lax
from jax.experimental import pallas as pl
from jax.experimental.pallas import tpu as pltpu
from jax.sharding import PartitionSpec as P

BF = jnp.bfloat16
F32 = jnp.float32
MESH = pl.DeviceIdType.MESH

D = 3584
HALF = D // 2
BLK = HALF // 2
WIN = 512
SLICE = 448
SLAB = 128
TOPK = 8
ROWS = 32
CAP = 6
SLOTS = 4 * CAP
CH = 4 * SLOTS
FAR = (2, 1, 3, 0)
PLACE = tuple((dx, (total - dx) % 4) for total in FAR for dx in FAR)
PART_A, PART_B = 512, 384
PARTS = ((0, PART_A), (2 * PART_A, PART_B))


def dot(a, b):
    return lax.dot_general(a, b, (((1,), (0,)), ((), ())), preferred_element_type=F32)


def dot_nt(a, b):
    return lax.dot_general(a, b, (((1,), (1,)), ((), ())), preferred_element_type=F32)


def iota(shape, dim):
    return lax.broadcasted_iota(jnp.int32, shape, dim)


def by24(q):
    return (q * 2731) >> 16


def by6(q):
    return (q * 10923) >> 16


def far(m):
    return jnp.where(m == 0, 2, jnp.where(m == 3, 0, 2 * m - 1))


def kernel(
    ro_t, rn_t, go_t, gn_t, rows_old, rows_new, w_old_hbm, w_new_hbm, w_out_hbm,
    out_old, out_new,
    tab_i, tab_f, result,
    w_raw, w_wide, w_old, w_new, w_out, square, meta_z, rz_old, rz_new, disp, comb,
    send_new, recv_new, send_old, recv_old, sib_old,
    pn, sx_send, sx_recv, rf_send, rf_recv, rn_send, rn_recv,
    po, so_send, so_recv, ra_send, ra_recv, rb_send, rb_recv,
    z1_own, z1_send, z1_recv, z2_send, z2_recv,
    ins, ws, zs, zr, xs, xr, fs, fr, sxs, sxr, rfs, rfr, rns, rnr, sos, sor, rts, rtr, z1s, z1r, z2s, z2r,
):
    ep = lax.axis_index("ep")
    rep = lax.axis_index("rep")
    core, zh = lax.rem(rep, 2), rep // 2
    zl, me = lax.rem(ep, 4), ep // 4
    x, y = me // 4, lax.rem(me, 4)
    z = zh * 4 + zl
    zoff = (1, 15, 2 + 12 * core)

    def z_dev(offset):
        t = lax.rem(z + offset, 16)
        return {"rep": (t // 4) * 2 + core, "ep": me * 4 + lax.rem(t, 4)}

    def to_dev(r):
        dx, dy = PLACE[r]
        return {"rep": rep, "ep": (lax.rem(x + dx, 4) * 4 + lax.rem(y + dy, 4)) * 4 + zl}

    def from_dev(r):
        dx, dy = PLACE[r]
        return {"rep": rep, "ep": (lax.rem(x + 4 - dx, 4) * 4 + lax.rem(y + 4 - dy, 4)) * 4 + zl}

    def zh_dev(k):
        return {"rep": lax.rem(zh + k, 4) * 2 + core, "ep": ep}

    sibling = {"rep": zh * 2 + (1 - core), "ep": ep}

    def remote(src, dst, ss, rs, dev):
        return pltpu.make_async_remote_copy(
            src_ref=src, dst_ref=dst, send_sem=ss, recv_sem=rs, device_id=dev, device_id_type=MESH
        )

    half = pl.multiple_of(core * HALF, 128)
    other = pl.multiple_of((1 - core) * HALF, 128)
    mine = pl.ds(pl.multiple_of(zl * ROWS, ROWS), ROWS)
    window = pl.ds(pl.multiple_of(zh * 896 + core * 384, 128), WIN)
    inputs = [
        pltpu.make_async_copy(src, dst, ins.at[i])
        for i, (src, dst) in enumerate(
            (
                (ro_t, tab_i.at[0]), (rn_t, tab_i.at[1]), (go_t, tab_f.at[0]), (gn_t, tab_f.at[1]),
                (rows_new.at[:, window], rz_new.at[mine, :]),
                (rows_old.at[:, pl.ds(half, HALF)], rz_old.at[mine, :]),
            )
        )
    ]
    for copy in inputs:
        copy.start()

    barrier = pltpu.get_barrier_semaphore()
    for r in range(15):
        pl.semaphore_signal(barrier, 1, device_id=to_dev(r), device_id_type=MESH)
    for o in (1, 15, 2, 14):
        pl.semaphore_signal(barrier, 1, device_id=z_dev(o), device_id_type=MESH)
    for k in range(1, 8):
        pl.semaphore_signal(
            barrier, 1, device_id={"rep": lax.rem(rep + k, 8), "ep": ep}, device_id_type=MESH
        )
    loads = [
        pltpu.make_async_copy(src, dst, ws.at[i])
        for i, (src, dst) in enumerate(
            ((w_new_hbm, w_raw.at[0]), (w_old_hbm, w_raw.at[1]), (w_out_hbm, w_out))
        )
    ]
    for load in loads:
        load.start()

    square[...] = jnp.zeros((128, 128), F32)
    for copy in inputs[:4]:
        copy.wait()
    for i, table in enumerate((tab_i.at[0], tab_i.at[1], tab_f.at[0], tab_f.at[1])):
        square[8 * i : 8 * i + 8, 0:ROWS] = table[...].astype(F32)
    meta_z[mine, :] = square[...].T[:ROWS, :]

    lane = iota((4 * ROWS, 128), 1)
    p_row, p_col = iota((4 * ROWS, 4 * ROWS), 0), iota((4 * ROWS, 4 * ROWS), 1)
    before = jnp.where((p_col < p_row) & (p_col >> 5 == p_row >> 5), 1.0, 0.0).astype(BF)
    qs = iota((16 * SLOTS, 128), 0)
    rq = by24(qs)
    dx = far(rq & 3)
    dy = (far(rq >> 2) - dx) & 3
    expert = (((x + dx) & 3) * 4 + ((y + dy) & 3)) * 4 + zl
    pick = jnp.where(expert == iota((16 * SLOTS, 128), 1), 1.0, 0.0).astype(BF)
    in_q = qs - by24(qs) * 24
    slot_q = (in_q - by6(in_q) * 6).astype(F32)
    same_q = by6(in_q) == iota((16 * SLOTS, 128), 1) >> 5
    ql = iota((128, 16 * SLOTS), 1)
    in_l = ql - by24(ql) * 24
    slot_l = (in_l - by6(in_l) * 6).astype(F32)
    same_l = by6(in_l) == iota((128, 16 * SLOTS), 0) >> 5
    pl.semaphore_wait(barrier, 26)

    def z_copy(o, kind):
        offset = zoff[o]
        there = lax.rem(z + offset, 16) // 4
        if kind == 0:
            src, land = meta_z.at[mine, :], meta_z
        elif kind == 1:
            theirs = pl.ds(pl.multiple_of(there * 896 + core * 384, 128), WIN)
            src, land = rows_new.at[:, theirs], rz_new
        else:
            src, land = rows_old.at[:, pl.ds(half, HALF)], rz_old
        return remote(src, land.at[mine, :], zs.at[kind, o], zr.at[kind, o], z_dev(offset))

    def z_from(o, kind, buf):
        src = lax.rem(zl + 16 - zoff[o], 4)
        ref = buf.at[pl.ds(pl.multiple_of(src * ROWS, ROWS), ROWS), :]
        return remote(ref, ref, zs.at[kind, o], zr.at[kind, o], z_dev(zoff[o]))

    for kind in range(3):
        for o in (2, 0, 1):
            z_copy(o, kind).start()
    for o in range(3):
        z_from(o, 0, meta_z).wait_recv()

    def tables(b):
        named = jnp.zeros((4 * ROWS, 128), F32)
        gate = jnp.zeros((4 * ROWS, 128), F32)
        for k in range(TOPK):
            hit = meta_z[:, 8 * b + k : 8 * b + k + 1].astype(jnp.int32) == lane
            named = named + jnp.where(hit, 1.0, 0.0)
            gate = gate + jnp.where(hit, meta_z[:, 16 + 8 * b + k : 17 + 8 * b + k], 0.0)
        rank = dot(before, named.astype(BF))
        code = jnp.where(named > 0.5, rank, -1.0).astype(BF)
        disp[b] = jnp.where((dot_nt(pick, code) == slot_q) & same_q, 1.0, 0.0).astype(BF)
        chosen = (dot_nt(code, pick) == slot_l) & same_l
        high = gate.astype(BF)
        low = (gate - high.astype(F32)).astype(BF)
        comb[b, 0] = jnp.where(chosen, dot_nt(high, pick), 0.0).astype(BF)
        comb[b, 1] = jnp.where(chosen, dot_nt(low, pick), 0.0).astype(BF)

    def message(b, buf, land, r):
        return remote(buf.at[r], land.at[r], xs.at[b, r // 4], xr.at[b, r // 4], to_dev(r))

    def others(n):
        return slice(4 * n, min(4 * n + 4, 15))

    def chunk(b, buf, land, n):
        at = others(n)
        return remote(buf.at[at], land.at[at], xs.at[b, n], xr.at[b, n], sibling)

    def put(buf, n, value, width):
        v = value.reshape(4, SLOTS, 2 * width)
        buf[4 * n : 4 * n + 4, 0:SLOTS, :] = v[:, :, :width].astype(BF)
        buf[4 * n : 4 * n + 4, SLOTS : 2 * SLOTS, :] = v[:, :, width:].astype(BF)

    def take(buf, n, h, width):
        v = buf[4 * n : 4 * n + 4, h * SLOTS : (h + 1) * SLOTS, :]
        return v.astype(F32).reshape(CH, width).astype(BF)

    def send_out(b, buf, land, n):
        for r in range(4 * n, 4 * n + 4):
            if r < 15:
                message(b, buf, land, r).start()
            else:
                land[15] = buf[15]

    def dispatch(b, rz, buf, land, width, ahead):
        for n in range(4):
            put(buf, n, dot(disp[b, n * CH : (n + 1) * CH, :], rz[...]), width)
            if n < ahead:
                send_out(b, buf, land, n)

    tables(1)
    for o in range(3):
        z_from(o, 1, rz_new).wait_recv()
    inputs[4].wait()
    dispatch(1, rz_new, send_new, recv_new, WIN // 2, 4)
    tables(0)
    for o in range(3):
        z_from(o, 2, rz_old).wait_recv()
    inputs[5].wait()
    dispatch(0, rz_old, send_old, recv_old, BLK, 2)

    loads[0].wait()
    w_wide[...] = w_raw[0].astype(F32)
    pad = WIN - SLICE
    w_new[:, pl.ds(pl.multiple_of((1 - core) * SLICE, 64), pad), :] = jnp.zeros((2, pad, 1024), BF)
    top = pl.ds(pl.multiple_of(core * pad, 64), SLICE)
    for h in range(8):
        for g in range(2):
            col = pl.multiple_of(lax.rem(h // 2 + 4 - zh, 4) * 256 + g * SLAB, SLAB)
            w_new[h % 2, top, pl.ds(col, SLAB)] = w_wide[pl.ds(2 * h + g, SLICE, stride=16), :].astype(BF)

    def sx_copy(n):
        return remote(sx_send.at[n], sx_recv.at[n], sxs.at[n], sxr.at[n], sibling)

    def rf_copy(n, i):
        return remote(rf_send.at[n, i], rf_recv.at[n, i], rfs.at[n, i], rfr.at[n, i], zh_dev(1 + 2 * i))

    def rn_copy(n, i):
        return remote(rn_send.at[n, i], rn_recv.at[n, i], rns.at[n, i], rnr.at[n, i], zh_dev(1 + 2 * i))

    def act_part(n):
        chunk(1, send_new, recv_new, n).wait_recv()
        rows = [take(recv_new, n, h, WIN // 2) for h in range(2)]

        def part(c):
            return sum(dot(rows[h], w_new[c, h * (WIN // 2) : (h + 1) * (WIN // 2), :]) for h in range(2))

        sx_send[n] = part(1 - core).astype(BF)
        sx_copy(n).start()
        pn[n] = part(core)

    def act_far(n):
        sx_copy(n).wait_recv()
        total = pn[n] + sx_recv[n].astype(F32)
        for i in range(2):
            rf_send[n, i] = total[i * CH // 2 : (i + 1) * CH // 2, 512:768].astype(BF)
            rf_copy(n, i).start()
        pn[n] = total

    def act_near(n):
        for i in range(2):
            rf_copy(n, i).wait_recv()
            cols = slice(256 + 512 * i, 512 + 512 * i)
            own, more = slice((1 - i) * CH // 2, (2 - i) * CH // 2), slice(i * CH // 2, (i + 1) * CH // 2)
            rn_send[n, i, own, :] = pn[n, own, cols].astype(BF)
            rn_send[n, i, more, :] = (pn[n, more, cols] + rf_recv[n, i].astype(F32)).astype(BF)
            rn_copy(n, i).start()

    def so_copy(b, n):
        return remote(so_send.at[b, n], so_recv.at[b, n], sos.at[b, n], sor.at[b, n], sibling)

    def down(b, n, act):
        gate = act[:, :SLAB]
        hidden = (gate / (1.0 + jnp.exp(-gate)) * act[:, SLAB:]).astype(BF)
        so_send[b, n] = dot(hidden, w_out[:, pl.ds(other, HALF)]).astype(BF)
        so_copy(b, n).start()
        po[b, n] = dot(hidden, w_out[:, pl.ds(half, HALF)])

    def back(b, part, r):
        src, land = ((ra_send, ra_recv), (rb_send, rb_recv))[part]
        return remote(src.at[b, r], land.at[b, r], rts.at[b, part], rtr.at[b, part], from_dev(r))

    def back_all(b, part):
        src, land = ((ra_send, ra_recv), (rb_send, rb_recv))[part]
        return remote(src.at[b, 0:15], land.at[b, 0:15], rts.at[b, part], rtr.at[b, part], sibling)

    def chip_sum(b, n):
        so_copy(b, n).wait_recv()
        total = po[b, n] + so_recv[b, n].astype(F32)
        put(ra_send.at[b], n, total[:, : 2 * PART_A], PART_A)
        put(rb_send.at[b], n, total[:, 2 * PART_A :], PART_B)

    def send_back(b, part, n):
        for r in range(4 * n, 4 * n + 4):
            if r < 15:
                back(b, part, r).start()
            elif part == 0:
                ra_recv[b, 15] = ra_send[b, 15]
            else:
                rb_recv[b, 15] = rb_send[b, 15]

    for n in range(5):
        if n < 4:
            act_part(n)
        if n >= 1:
            act_far(n - 1)

    for n in range(2, 4):
        chunk(0, send_old, recv_old, n - 2).wait_send()
        send_out(0, send_old, recv_old, n)

    def fwd_copy(n):
        at = slice(4 * n, 4 * n + 4)
        return remote(recv_old.at[at], sib_old.at[at], fs.at[n], fr.at[n], sibling)

    def forward(n):
        chunk(0, send_old, recv_old, n).wait_recv()
        fwd_copy(n).start()

    def act_old(n):
        act = jnp.zeros((CH, 2 * SLAB), F32)
        for h in range(2):
            at = pl.ds(pl.multiple_of(half + h * BLK, 128), BLK)
            act += dot(take(recv_old, n, h, BLK), w_old[at, :])
        fwd_copy(n).wait_recv()
        for h in range(2):
            at = pl.ds(pl.multiple_of(other + h * BLK, 128), BLK)
            act += dot(take(sib_old, n, h, BLK), w_old[at, :])
        down(0, n, act)

    loads[1].wait()
    w_wide[...] = w_raw[1].astype(F32)
    for g in range(2):
        w_old[:, g * SLAB : (g + 1) * SLAB] = w_wide[pl.ds(g, D, stride=2), :].astype(BF)
    loads[2].wait()

    for n in range(6):
        if n < 4:
            forward(n)
            act_near(n)
        if 1 <= n < 5:
            act_old(n - 1)
        if n >= 2:
            chip_sum(0, n - 2)
            send_back(0, 0, n - 2)
            send_back(0, 1, n - 2)

    def act_new(n):
        act = pn[n, :, 0:256]
        for i in range(2):
            rn_copy(n, i).wait_recv()
            act += rn_recv[n, i].astype(F32)
        down(1, n, act)

    for n in range(5):
        if n < 4:
            act_new(n)
        if 1 <= n < 5:
            chip_sum(1, n - 1)
            send_back(1, 0, n - 1)

    for n in range(4):
        send_back(1, 1, n)

    def z1_copy(b, part, o):
        at = pl.ds(pl.multiple_of(lax.rem(zl + zoff[o], 4) * ROWS, ROWS), ROWS)
        col, width = PARTS[part]
        cols = slice(col, col + 2 * width)
        return remote(
            z1_send.at[b, at, cols], z1_recv.at[b, o, :, cols],
            z1s.at[b, part, o], z1r.at[b, part, o], z_dev(zoff[o]),
        )

    def combine(b, part):
        back_all(b, part).wait_recv()
        col, width = PARTS[part]
        for h in range(2):
            rows = (ra_recv, rb_recv)[part][b, :, h * SLOTS : (h + 1) * SLOTS, :]
            rows = rows.astype(F32).reshape(16 * SLOTS, width).astype(BF)
            total = dot(comb[b, 0], rows) + dot(comb[b, 1], rows)
            cols = slice(col + h * width, col + (h + 1) * width)
            z1_own[b, :, cols] = total
            z1_send[b, :, cols] = total.astype(BF)
        for o in (2, 0, 1):
            z1_copy(b, part, o).start()

    def z2_copy(b, t):
        k, c = t // 2, t % 2
        return remote(
            z2_send.at[b, :, k * 896 + c * 384 : k * 896 + c * 384 + WIN], z2_recv.at[b, zh],
            z2s.at[b, t], z2r.at[b, zh], {"rep": (2 * core + k) * 2 + c, "ep": ep},
        )

    def is_self(t):
        return rep == (2 * core + t // 2) * 2 + t % 2

    def spread(b, part):
        col, width = PARTS[part]
        cols = slice(col, col + 2 * width)
        total = z1_own[b, mine, cols]
        for o in range(3):
            z1_copy(b, part, o).wait_recv()
            total += z1_recv[b, o, :, cols].astype(F32)
        z2_send[b, :, cols] = total.astype(BF)
        for t in (2 * part, 2 * part + 1):
            k, c = t // 2, t % 2

            @pl.when(jnp.logical_not(is_self(t)))
            def _():
                z2_copy(b, t).start()

            @pl.when(is_self(t))
            def _():
                z2_recv[b, zh] = z2_send[b, :, k * 896 + c * 384 : k * 896 + c * 384 + WIN]

    def finish(b, out):
        for s in range(4):

            @pl.when(jnp.logical_not((zh == s) & (core == zh // 2)))
            def _():
                ref = z2_recv.at[b, s]
                remote(ref, ref, z2s.at[b, 0], z2r.at[b, s], sibling).wait_recv()

        total = sum(z2_recv[b, s].astype(F32) for s in range(4))
        result[b] = jnp.where(core == 0, total[:, :SLICE], total[:, WIN - SLICE :])
        pltpu.make_async_copy(result.at[b], out, ins.at[b]).start()

    combine(0, 0)
    combine(0, 1)
    spread(0, 0)
    spread(0, 1)
    combine(1, 0)
    combine(1, 1)
    spread(1, 0)
    spread(1, 1)
    finish(0, out_old)
    finish(1, out_new)

    for b, out in enumerate((out_old, out_new)):
        pltpu.make_async_copy(result.at[b], out, ins.at[b]).wait()

    for o in range(3):
        for kind in range(3):
            z_copy(o, kind).wait_send()
        for b in range(2):
            for part in range(2):
                z1_copy(b, part, o).wait_send()
    for n in range(4):
        sx_copy(n).wait_send()
        for i in range(2):
            rf_copy(n, i).wait_send()
            rn_copy(n, i).wait_send()
        for b in range(2):
            so_copy(b, n).wait_send()
    for b in range(2):
        for part in range(2):
            back_all(b, part).wait_send()
    for n in range(4):
        fwd_copy(n).wait_send()
        if n >= 2:
            chunk(0, send_old, recv_old, n).wait_send()
        chunk(1, send_new, recv_new, n).wait_send()
    for b in range(2):
        for t in range(4):

            @pl.when(jnp.logical_not(is_self(t)))
            def _():
                z2_copy(b, t).wait_send()


def body(rows_old, rows_new, routes_old, routes_new, gates_old, gates_new, w_in_old, w_in_new, w_out):
    w_old = w_in_old[0].reshape(2 * D, SLAB)
    w_new = w_in_new[0].reshape(SLICE, 2, 8, SLAB).transpose(0, 2, 1, 3).reshape(SLICE * 16, SLAB)
    hbm = pl.BlockSpec(memory_space=pl.ANY)
    dma = pltpu.SemaphoreType.DMA
    out = jax.ShapeDtypeStruct((ROWS, SLICE), F32)
    old, new = pl.pallas_call(
        kernel,
        out_shape=(out, out),
        in_specs=[hbm] * 9,
        out_specs=(hbm, hbm),
        scratch_shapes=[
            pltpu.VMEM((2, TOPK, ROWS), jnp.int32),
            pltpu.VMEM((2, TOPK, ROWS), F32),
            pltpu.VMEM((2, ROWS, SLICE), F32),
            pltpu.VMEM((2, 2 * D, SLAB), BF),
            pltpu.VMEM((2 * D, SLAB), F32),
            pltpu.VMEM((D, 2 * SLAB), BF),
            pltpu.VMEM((2, WIN, 1024), BF),
            pltpu.VMEM((SLAB, D), BF),
            pltpu.VMEM((128, 128), F32),
            pltpu.VMEM((4 * ROWS, 128), F32),
            pltpu.VMEM((4 * ROWS, HALF), BF),
            pltpu.VMEM((4 * ROWS, WIN), BF),
            pltpu.VMEM((2, 16 * SLOTS, 128), BF),
            pltpu.VMEM((2, 2, 128, 16 * SLOTS), BF),
            pltpu.VMEM((16, 2 * SLOTS, WIN // 2), BF),
            pltpu.VMEM((16, 2 * SLOTS, WIN // 2), BF),
            pltpu.VMEM((16, 2 * SLOTS, BLK), BF),
            pltpu.VMEM((16, 2 * SLOTS, BLK), BF),
            pltpu.VMEM((16, 2 * SLOTS, BLK), BF),
            pltpu.VMEM((4, CH, 1024), F32),
            pltpu.VMEM((4, CH, 1024), BF),
            pltpu.VMEM((4, CH, 1024), BF),
            pltpu.VMEM((4, 2, CH // 2, 256), BF),
            pltpu.VMEM((4, 2, CH // 2, 256), BF),
            pltpu.VMEM((4, 2, CH, 256), BF),
            pltpu.VMEM((4, 2, CH, 256), BF),
            pltpu.VMEM((2, 4, CH, HALF), F32),
            pltpu.VMEM((2, 4, CH, HALF), BF),
            pltpu.VMEM((2, 4, CH, HALF), BF),
            pltpu.VMEM((2, 16, 2 * SLOTS, PART_A), BF),
            pltpu.VMEM((2, 16, 2 * SLOTS, PART_A), BF),
            pltpu.VMEM((2, 16, 2 * SLOTS, PART_B), BF),
            pltpu.VMEM((2, 16, 2 * SLOTS, PART_B), BF),
            pltpu.VMEM((2, 4 * ROWS, HALF), F32),
            pltpu.VMEM((2, 4 * ROWS, HALF), BF),
            pltpu.VMEM((2, 3, ROWS, HALF), BF),
            pltpu.VMEM((2, ROWS, HALF), BF),
            pltpu.VMEM((2, 4, ROWS, WIN), BF),
            dma((6,)),
            dma((3,)),
            dma((3, 3)), dma((3, 3)),
            dma((2, 4)), dma((2, 4)),
            dma((4,)), dma((4,)),
            dma((4,)), dma((4,)),
            dma((4, 2)), dma((4, 2)),
            dma((4, 2)), dma((4, 2)),
            dma((2, 4)), dma((2, 4)),
            dma((2, 2)), dma((2, 2)),
            dma((2, 2, 3)), dma((2, 2, 3)),
            dma((2, 4)), dma((2, 4)),
        ],
        compiler_params=pltpu.CompilerParams(
            collective_id=0, has_side_effects=True, vmem_limit_bytes=60 * 1024 * 1024
        ),
    )(routes_old.T, routes_new.T, gates_old.T, gates_new.T, rows_old, rows_new, w_old, w_new, w_out[0])
    return old.astype(BF), new.astype(BF)


def solution(mesh):
    return jax.shard_map(
        body,
        mesh=mesh,
        in_specs=(
            P("ep", None),
            P("ep", None),
            P("ep", None),
            P("ep", None),
            P("ep", None),
            P("ep", None),
            P("ep", None, None, "rep"),
            P("ep", "rep", None, None),
            P("ep", "rep", None),
        ),
        out_specs=(P("ep", "rep"), P("ep", "rep")),
        check_vma=False,
    )
```
